256 devices in a mesh: ctx: 64 (over z, y, core), kvh: 4 (over x).
Axes of the slice: x: 4, y: 4, z: 8, core: 2. Of those that a mesh axis runs over, the one named last changes fastest.
Arguments:
- tokens: bfloat16 [32768, 4096], P('ctx', 'kvh'), may hold values from -6 to 6
- norm_gain: float32 [4096], replicated, may hold values from 0.1 to 1.9
- w_query: bfloat16 [4096, 2048], P(None, 'kvh'), may hold values from -0.09375 to 0.09375
- w_key: bfloat16 [4096, 512], P(None, 'kvh'), may hold values from -0.09375 to 0.09375
- w_value: bfloat16 [4096, 512], P(None, 'kvh'), may hold values from -0.09375 to 0.09375
- w_out: bfloat16 [2048, 4096], P('kvh'), may hold values from -0.125 to 0.125
- picks: int32 [64, 4, 3], P('ctx', 'kvh'), may hold values from 0 to 62, as said below
Outputs:
- combined: bfloat16 [32768, 4096], P(('ctx', 'kvh'))
The draws below stay inside these ranges and needn't reach their ends.
Inputs may be any that keep to these rules, and one draw needn't show every extreme that they name: `picks`: for block b > 0 and each KV head the 3 entries, where below b, are distinct, the first being b - 1; for b < 3 the entries that find no earlier block equal b and choose nothing.
All inputs are finite; a program needn't handle non-finite values.
Results may differ from the reference program's by a relative error of at most 0.018.
Values may be sent and summed in bfloat16 or wider, within the bound.
No kernel may reach another device: no remote copies, remote signals or barrier semaphores. Data moves between devices by JAX's collectives and lax.ppermute only.
A program may use at most 128 MiB of HBM per device.

```python
import jax
import jax.numpy as jnp
from jax import lax

D = 4096
HD = 128
QPK = 4
BLOCK = 512
TOPK = 3
KVHEADS = 4
QHEADS = 16
NBLK = 64
TOKENS = 32768


def draw_picks(key, part):
    key = jax.random.fold_in(key, 7)
    raw_scores = jax.random.randint(key, (NBLK, KVHEADS, NBLK), 0, 1 << 20)
    columns = jnp.arange(NBLK, dtype=jnp.int32)[None, None, :]
    row_ids = jnp.arange(NBLK, dtype=jnp.int32)[:, None, None]
    distinct = raw_scores * NBLK + columns
    keyed = jnp.where(columns < row_ids, distinct, -1 - columns)
    keyed = jnp.where(columns == row_ids - 1, jnp.int32(1 << 28), keyed)
    ranked, chosen = lax.top_k(keyed, TOPK)
    chosen = chosen.astype(jnp.int32)
    return jnp.where(chosen < row_ids, chosen, row_ids).astype(jnp.int32)


def levels(stream_key, dims, split, low, top_value):
    loudness, own = 1.0, jax.random.fold_in(stream_key, 6)
    for dim, shards_of in split:
        draws = jnp.exp(jax.random.uniform(jax.random.fold_in(own, dim), (shards_of,), jnp.float32, low / len(split), top_value / len(split)))
        loudness = loudness * jnp.repeat(draws, dims[dim] // shards_of).reshape([-1 if axis == dim else 1 for axis in range(len(dims))])
    return loudness


def noise(rng, extent, scale, most, cuts=(), kind=jnp.bfloat16):
    gain = levels(rng, extent, cuts, -0.22, 0.18) if cuts else 1.0
    entries = jax.random.normal(rng, extent, jnp.float32) * scale * gain
    return jnp.minimum(jnp.maximum(entries, -most), most).astype(kind)


def setup_inputs(seed: int = 0) -> dict:
    keys = jax.random.split(jax.random.key(seed), 8)
    return {
        "tokens": noise(keys[0], (TOKENS, D), 1.0, 6.0, ((0, 64), (1, 4))),
        "norm_gain": jnp.clip(1.0 + 0.18 * jax.random.normal(keys[1], (D,), jnp.float32), 0.1, 1.9),
        "w_query": noise(keys[2], (D, QHEADS * HD), D ** -0.5, 0.09375, ((1, 4),)),
        "w_key": noise(keys[3], (D, KVHEADS * HD), D ** -0.5, 0.09375, ((1, 4),)),
        "w_value": noise(keys[4], (D, KVHEADS * HD), D ** -0.5, 0.09375, ((1, 4),)),
        "w_out": noise(keys[5], (QHEADS * HD, D), (QHEADS * HD) ** -0.5, 0.125, ((0, 4),)),
        "picks": draw_picks(jax.random.fold_in(keys[7], 71), 0),
    }


ROPE_BASE = 500000.0

def rotate_pairs(head_rows, positions):
    half_dim = head_rows.shape[-1] // 2
    frequency = ROPE_BASE ** (-jnp.arange(half_dim, dtype=jnp.float32) * 2.0 / head_rows.shape[-1])
    angles = positions.astype(jnp.float32)[:, None] * frequency[None, :]
    cosine = jnp.cos(angles)[:, None, :]
    sine_part = jnp.sin(angles)[:, None, :]
    lower_half = head_rows[..., :half_dim]
    upper_half = head_rows[..., half_dim:]
    return jnp.concatenate([lower_half * cosine - upper_half * sine_part, upper_half * cosine + lower_half * sine_part], axis=-1)

def normalize(token_rows, norm_gain):
    wide_rows = token_rows.astype(jnp.float32)
    square_mean = lax.optimization_barrier(jnp.mean(wide_rows * wide_rows, axis=-1, keepdims=True))
    return (wide_rows * lax.rsqrt(square_mean + 1e-05) * norm_gain.astype(jnp.float32)).astype(jnp.bfloat16)

def attend(query_tokens, blocked_keys, blocked_values, usable):
    block_len = query_tokens.shape[0]
    block_scores = jnp.einsum('sef,wpf->eswp', query_tokens.astype(jnp.float32), blocked_keys.astype(jnp.float32)) * query_tokens.shape[-1] ** (-0.5)
    causal = jnp.arange(block_len)[:, None] >= jnp.arange(block_len)[None, :]
    far_allowed = jnp.broadcast_to(usable[None, :, None], (block_len, usable.shape[0], block_len))
    allowed = jnp.concatenate([causal[:, None, :], far_allowed], axis=1)
    weights = jnp.where(allowed[None], jnp.exp(block_scores), jnp.float32(0.0))
    totals = lax.optimization_barrier(jnp.sum(weights, axis=(2, 3), keepdims=True))
    share_weights = (weights / totals).astype(jnp.bfloat16)
    attended_output = jnp.einsum('pcxy,xyf->cpf', share_weights.astype(jnp.float32), blocked_values.astype(jnp.float32))
    return attended_output.astype(jnp.bfloat16).reshape(block_len, -1)

def reference(tokens, norm_gain, w_query, w_key, w_value, w_out, picks):
    token_blocks = tokens.reshape(NBLK, BLOCK, D)
    block_ids = jnp.arange(NBLK, dtype=jnp.int32)

    def project_kv(inputs):
        block_rows, block_index = inputs
        normed = normalize(block_rows, norm_gain)
        positions = block_index * BLOCK + jnp.arange(BLOCK, dtype=jnp.int32)
        key_rows = jnp.dot(normed, w_key, preferred_element_type=jnp.float32).reshape(BLOCK, KVHEADS, HD)
        key_rows = rotate_pairs(key_rows, positions).astype(jnp.bfloat16)
        value_rows = jnp.dot(normed, w_value, preferred_element_type=jnp.float32).astype(jnp.bfloat16).reshape(BLOCK, KVHEADS, HD)
        return (key_rows, value_rows)
    key_all, value_all = lax.map(project_kv, (token_blocks, block_ids))
    key_heads = jnp.transpose(key_all, (2, 0, 1, 3))
    value_heads = jnp.transpose(value_all, (2, 0, 1, 3))

    def one_block(inputs):
        block_rows, block_index = inputs
        normed = normalize(block_rows, norm_gain)
        positions = block_index * BLOCK + jnp.arange(BLOCK, dtype=jnp.int32)
        query_tokens = jnp.dot(normed, w_query, preferred_element_type=jnp.float32).reshape(BLOCK, QHEADS, HD)
        query_tokens = rotate_pairs(query_tokens, positions).astype(jnp.bfloat16).reshape(BLOCK, KVHEADS, QPK, HD)
        chosen = lax.dynamic_index_in_dim(picks, block_index, 0, keepdims=False)

        def one_group(group_query, group_keys, group_values, group_chosen):
            own_keys = lax.dynamic_index_in_dim(group_keys, block_index, 0, keepdims=True)
            own_values = lax.dynamic_index_in_dim(group_values, block_index, 0, keepdims=True)
            blocked_keys = jnp.concatenate([own_keys, group_keys[group_chosen]], axis=0)
            blocked_values = jnp.concatenate([own_values, group_values[group_chosen]], axis=0)
            return attend(group_query, blocked_keys, blocked_values, group_chosen < block_index)
        grouped = jax.vmap(one_group, in_axes=(1, 0, 0, 0), out_axes=1)(query_tokens, key_heads, value_heads, chosen)
        attended_output = grouped.reshape(BLOCK, QHEADS * HD)
        return jnp.dot(attended_output, w_out, preferred_element_type=jnp.float32).astype(jnp.bfloat16)
    combined = lax.map(one_block, (token_blocks, block_ids))
    return combined.reshape(TOKENS, D)
```

```python
import jax
import jax.numpy as jnp
from jax import lax
from jax.sharding import PartitionSpec as P

HD = 128


ROPE_BASE = 500000.0


def rotate_pairs(head_rows, positions):
    half_dim = head_rows.shape[-1] // 2
    frequency = ROPE_BASE ** (-jnp.arange(half_dim, dtype=jnp.float32) * 2.0 / head_rows.shape[-1])
    angles = positions.astype(jnp.float32)[:, None] * frequency[None, :]
    cosine = jnp.cos(angles)[:, None, :]
    sine_part = jnp.sin(angles)[:, None, :]
    lower_half = head_rows[..., :half_dim]
    upper_half = head_rows[..., half_dim:]
    return jnp.concatenate(
        [
            lower_half * cosine - upper_half * sine_part,
            upper_half * cosine + lower_half * sine_part,
        ],
        axis=-1,
    )


def normalize(token_rows, norm_gain):
    wide_rows = token_rows.astype(jnp.float32)
    square_mean = jnp.mean(wide_rows * wide_rows, axis=-1, keepdims=True)
    return (wide_rows * lax.rsqrt(square_mean + 1e-05) * norm_gain).astype(jnp.bfloat16)


def attend(query_tokens, blocked_keys, blocked_values, usable):
    block_len = query_tokens.shape[0]
    block_scores = jnp.einsum(
        "sef,wpf->eswp", query_tokens, blocked_keys, preferred_element_type=jnp.float32
    ) * query_tokens.shape[-1] ** (-0.5)
    causal = jnp.arange(block_len)[:, None] >= jnp.arange(block_len)[None, :]
    far_allowed = jnp.broadcast_to(usable[None, :, None], (block_len, usable.shape[0], block_len))
    allowed = jnp.concatenate([causal[:, None, :], far_allowed], axis=1)
    weights = jnp.where(allowed[None], jnp.exp(block_scores), jnp.float32(0.0))
    totals = jnp.sum(weights, axis=(2, 3), keepdims=True)
    share_weights = (weights / totals).astype(jnp.bfloat16)
    attended_output = jnp.einsum(
        "pcxy,xyf->cpf", share_weights, blocked_values, preferred_element_type=jnp.float32
    )
    return attended_output.astype(jnp.bfloat16).reshape(block_len, -1)


def local(tokens, norm_gain, w_query, w_key, w_value, w_out, picks):
    features = lax.all_gather(tokens, "kvh", axis=1, tiled=True)
    normed = normalize(features, norm_gain)
    block_len = features.shape[0]
    block_index = lax.axis_index("ctx")
    positions = block_index * block_len + jnp.arange(block_len, dtype=jnp.int32)
    query_tokens = jnp.dot(normed, w_query, preferred_element_type=jnp.float32).reshape(
        block_len, -1, HD
    )
    query_tokens = rotate_pairs(query_tokens, positions).astype(jnp.bfloat16)
    key_rows = jnp.dot(normed, w_key, preferred_element_type=jnp.float32).reshape(block_len, 1, HD)
    key_rows = rotate_pairs(key_rows, positions)[:, 0].astype(jnp.bfloat16)
    value_rows = jnp.dot(normed, w_value, preferred_element_type=jnp.float32).astype(jnp.bfloat16)
    chosen = picks[0, 0]
    ctx_count = lax.axis_size("ctx")
    pieces = ctx_count // 2
    wanted = lax.all_to_all(
        jnp.broadcast_to(chosen[None, None, 1:], (ctx_count, 1, 2)), "ctx", 0, 0
    ).reshape(ctx_count * 2)
    own = jnp.concatenate([key_rows, value_rows], axis=0)
    held = lax.all_to_all(own.reshape(ctx_count, -1, HD), "ctx", 0, 0)
    before = lax.ppermute(own, "ctx", [(i, i + 1) for i in range(ctx_count - 1)])
    sent = held[wanted].reshape(ctx_count, 2, -1, HD)
    got = lax.all_to_all(sent, "ctx", 0, 0)
    far_keys = jnp.moveaxis(got[:pieces], 1, 0).reshape(2, block_len, HD)
    far_values = jnp.moveaxis(got[pieces:], 1, 0).reshape(2, block_len, HD)
    blocked_keys = jnp.concatenate([key_rows[None], before[None, :block_len], far_keys], axis=0)
    blocked_values = jnp.concatenate([value_rows[None], before[None, block_len:], far_values], axis=0)
    attended_output = attend(query_tokens, blocked_keys, blocked_values, chosen < block_index)
    return lax.psum_scatter(
        jnp.dot(attended_output, w_out, preferred_element_type=jnp.float32).astype(jnp.bfloat16),
        "kvh",
        scatter_dimension=0,
        tiled=True,
    )


def solution(mesh):
    in_specs = (
        P("ctx", "kvh"),
        P(),
        P(None, "kvh"),
        P(None, "kvh"),
        P(None, "kvh"),
        P("kvh", None),
        P("ctx", "kvh", None),
    )
    out_specs = P(("ctx", "kvh"), None)
    return jax.shard_map(local, mesh=mesh, in_specs=in_specs, out_specs=out_specs, check_vma=False)
```

```python
import jax
import jax.numpy as jnp
from jax import lax
from jax.sharding import PartitionSpec as P

HD = 128


ROPE_BASE = 500000.0


def rotate_pairs(head_rows, positions):
    half_dim = head_rows.shape[-1] // 2
    frequency = ROPE_BASE ** (-jnp.arange(half_dim, dtype=jnp.float32) * 2.0 / head_rows.shape[-1])
    angles = positions.astype(jnp.float32)[:, None] * frequency[None, :]
    cosine = jnp.cos(angles)[:, None, :]
    sine_part = jnp.sin(angles)[:, None, :]
    lower_half = head_rows[..., :half_dim]
    upper_half = head_rows[..., half_dim:]
    return jnp.concatenate(
        [
            lower_half * cosine - upper_half * sine_part,
            upper_half * cosine + lower_half * sine_part,
        ],
        axis=-1,
    )


def attend(query_tokens, blocked_keys, blocked_values, usable):
    block_len = query_tokens.shape[0]
    block_scores = jnp.einsum(
        "sef,wpf->eswp", query_tokens, blocked_keys, preferred_element_type=jnp.float32
    ) * query_tokens.shape[-1] ** (-0.5)
    causal = jnp.arange(block_len)[:, None] >= jnp.arange(block_len)[None, :]
    far_allowed = jnp.broadcast_to(usable[None, :, None], (block_len, usable.shape[0], block_len))
    allowed = jnp.concatenate([causal[:, None, :], far_allowed], axis=1)
    weights = jnp.where(allowed[None], jnp.exp(block_scores), jnp.float32(0.0))
    totals = jnp.sum(weights, axis=(2, 3), keepdims=True)
    share_weights = (weights / totals).astype(jnp.bfloat16)
    attended_output = jnp.einsum(
        "pcxy,xyf->cpf", share_weights, blocked_values, preferred_element_type=jnp.float32
    )
    return attended_output.astype(jnp.bfloat16).reshape(block_len, -1)


RING = 4
RIGHT = [(i, (i + 1) % RING) for i in range(RING)]
LEFT = [(i, (i - 1) % RING) for i in range(RING)]
EVEN = [(i, i ^ 1) for i in range(RING)]
ODD = [(i, RING - 1 - i) for i in range(RING)]


def gather_features(own, me):
    rows, width = own.shape
    half = rows // 2
    from_left = lax.ppermute(own, "kvh", RIGHT)
    from_right = lax.ppermute(own, "kvh", LEFT)
    upper = lax.ppermute(from_left[:half], "kvh", RIGHT)
    lower = lax.ppermute(from_right[half:], "kvh", LEFT)
    wide = jnp.zeros((rows, RING * width), own.dtype)
    wide = lax.dynamic_update_slice(wide, own, (0, me * width))
    wide = lax.dynamic_update_slice(wide, from_left, (0, (me + 3) % RING * width))
    wide = lax.dynamic_update_slice(wide, from_right, (0, (me + 1) % RING * width))
    across = (me + 2) % RING * width
    wide = lax.dynamic_update_slice(wide, upper, (0, across))
    wide = lax.dynamic_update_slice(wide, lower, (half, across))
    return wide, (from_left, from_right)


def project_out(attended, w_out, w_near, me):
    rows, depth = attended.shape
    quarter, half = rows // RING, w_out.shape[1] // 2
    even, odd = me ^ 1, RING - 1 - me
    parts = attended.reshape(RING, quarter, depth)

    def pick(one, two):
        return jnp.concatenate(
            [
                lax.dynamic_index_in_dim(parts, one, 0, keepdims=False),
                lax.dynamic_index_in_dim(parts, two, 0, keepdims=False),
            ],
            axis=0,
        )

    across = (me + 2) % RING
    got_even = lax.ppermute(pick(even, across), "kvh", EVEN)
    got_odd = lax.ppermute(pick(odd, across), "kvh", ODD)
    first = jnp.concatenate([pick(me, odd), got_even], axis=1)
    second = jnp.concatenate([pick(me, even), got_odd], axis=1)
    w_first = jnp.concatenate([w_out[:, :half], w_near[:, :half]], axis=0)
    w_second = jnp.concatenate([w_out[:, half:], w_near[:, half:]], axis=0)
    sums_first = jnp.dot(first, w_first, preferred_element_type=jnp.float32)
    sums_second = jnp.dot(second, w_second, preferred_element_type=jnp.float32)
    other_first = lax.ppermute(sums_first[quarter:].astype(jnp.bfloat16), "kvh", ODD)
    other_second = lax.ppermute(sums_second[quarter:].astype(jnp.bfloat16), "kvh", EVEN)
    return jnp.concatenate(
        [
            (sums_first[:quarter] + other_first.astype(jnp.float32)).astype(jnp.bfloat16),
            (sums_second[:quarter] + other_second.astype(jnp.float32)).astype(jnp.bfloat16),
        ],
        axis=1,
    )


def local(tokens, norm_gain, w_query, w_key, w_value, w_out, picks):
    me, block_index = lax.axis_index("kvh"), lax.axis_index("ctx")
    ctx_count = lax.axis_size("ctx")
    block_len = tokens.shape[0]
    half, pieces = block_len // 2, ctx_count // 2
    chosen = picks[0, 0]

    share = w_out.shape[0] // ctx_count
    passed = lax.dynamic_slice_in_dim(w_out, block_index * share, share, 0)
    mid = w_out.shape[1] // 2
    w_near = lax.all_gather(
        jnp.concatenate(
            [lax.ppermute(passed[:, :mid], "kvh", EVEN), lax.ppermute(passed[:, mid:], "kvh", ODD)],
            axis=1,
        ),
        "ctx",
        axis=0,
        tiled=True,
    )

    wanted = lax.all_to_all(
        jnp.broadcast_to(chosen[None, None, 1:], (ctx_count, 1, 2)), "ctx", 0, 0
    ).reshape(ctx_count * 2)

    gain = norm_gain[:, None]
    w_kv = (jnp.concatenate([w_key, w_value], axis=1) * gain).astype(jnp.bfloat16)
    w_q = (w_query * gain).astype(jnp.bfloat16)
    positions = block_index * block_len + jnp.arange(block_len, dtype=jnp.int32)

    def project(wide, place):
        square_mean = jnp.mean(jnp.square(wide.astype(jnp.float32)), axis=-1, keepdims=True)
        scale = lax.rsqrt(square_mean + 1e-05)
        kv = jnp.dot(wide, w_kv, preferred_element_type=jnp.float32) * scale
        key_rows = rotate_pairs(kv[:, None, :HD], place)[:, 0].astype(jnp.bfloat16)
        return key_rows, kv[:, HD:].astype(jnp.bfloat16), scale

    def spread(key_rows, value_rows):
        own = jnp.concatenate([key_rows, value_rows], axis=0)
        return lax.all_to_all(own.reshape(ctx_count, -1, HD), "ctx", 0, 0)

    top, landed = gather_features(tokens[:half], me)
    rest, landed, wanted = lax.optimization_barrier((tokens[half:], landed, wanted))
    bottom, _ = gather_features(rest, me)
    key_top, value_top, scale_top = project(top, positions[:half])
    held_top = spread(key_top, value_top)
    key_bottom, value_bottom, scale_bottom = project(bottom, positions[half:])
    held_bottom = spread(key_bottom, value_bottom)
    held = jnp.concatenate([held_top, held_bottom], axis=1)
    got = lax.all_to_all(held[wanted].reshape(ctx_count, 2, -1, HD), "ctx", 0, 0)
    own = jnp.concatenate([key_top, key_bottom, value_top, value_bottom], axis=0)
    before = lax.ppermute(own, "ctx", [(i, i + 1) for i in range(ctx_count - 1)])

    query_tokens = jnp.concatenate(
        [
            jnp.dot(top, w_q, preferred_element_type=jnp.float32) * scale_top,
            jnp.dot(bottom, w_q, preferred_element_type=jnp.float32) * scale_bottom,
        ],
        axis=0,
    ).reshape(block_len, -1, HD)
    query_tokens = rotate_pairs(query_tokens, positions).astype(jnp.bfloat16)
    far_keys = jnp.moveaxis(got[:pieces], 1, 0).reshape(2, block_len, HD)
    far_values = jnp.moveaxis(got[pieces:], 1, 0).reshape(2, block_len, HD)
    blocked_keys = jnp.concatenate(
        [own[None, :block_len], before[None, :block_len], far_keys], axis=0
    )
    blocked_values = jnp.concatenate(
        [own[None, block_len:], before[None, block_len:], far_values], axis=0
    )
    attended = attend(query_tokens, blocked_keys, blocked_values, chosen < block_index)
    return project_out(attended, w_out, w_near, me)


def solution(mesh):
    in_specs = (
        P("ctx", "kvh"),
        P(),
        P(None, "kvh"),
        P(None, "kvh"),
        P(None, "kvh"),
        P("kvh", None),
        P("ctx", "kvh", None),
    )
    out_specs = P(("ctx", "kvh"), None)
    return jax.shard_map(local, mesh=mesh, in_specs=in_specs, out_specs=out_specs, check_vma=False)
```

```python
import jax
import jax.numpy as jnp
from jax import lax
from jax.experimental import pallas as pl
from jax.experimental.pallas import tpu as pltpu
from jax.sharding import PartitionSpec as P

HD = 128


ROPE_BASE = 500000.0


def rotate_pairs(head_rows, positions):
    half_dim = head_rows.shape[-1] // 2
    frequency = ROPE_BASE ** (-jnp.arange(half_dim, dtype=jnp.float32) * 2.0 / head_rows.shape[-1])
    angles = positions.astype(jnp.float32)[:, None] * frequency[None, :]
    cosine = jnp.cos(angles)[:, None, :]
    sine_part = jnp.sin(angles)[:, None, :]
    lower_half = head_rows[..., :half_dim]
    upper_half = head_rows[..., half_dim:]
    return jnp.concatenate(
        [
            lower_half * cosine - upper_half * sine_part,
            upper_half * cosine + lower_half * sine_part,
        ],
        axis=-1,
    )


LOG2E = 1.4426950408889634
MASKED = -1e30


def stack_heads(rows):
    return jnp.concatenate(
        [rows[:, h * HD : (h + 1) * HD] for h in range(rows.shape[1] // HD)], axis=0
    )


def scores_of(queries, keys):
    return lax.dot_general(
        queries, keys, (((1,), (1,)), ((), ())), preferred_element_type=jnp.float32
    )


def weigh(scores, top, values):
    weights = jnp.exp2((scores - top) * (LOG2E * HD**-0.5)).astype(jnp.bfloat16)
    wide = jnp.concatenate([values, jnp.ones_like(values)], axis=1)
    return jnp.dot(weights, wide, preferred_element_type=jnp.float32)


def near_kernel(flag_ref, query_ref, own_ref, before_ref, sums_ref, top_ref):
    block_len = query_ref.shape[0]
    quarter = block_len // RING
    heads = query_ref.shape[1] // HD
    stacked = quarter * heads
    has_before = flag_ref[0] > 0
    for c in range(RING):
        span = (c + 1) * quarter
        queries = stack_heads(query_ref[c * quarter : span, :])
        own_scores = scores_of(queries, own_ref[:span, :])
        row = lax.broadcasted_iota(jnp.int32, (stacked, span), 0) % quarter + c * quarter
        column = lax.broadcasted_iota(jnp.int32, (stacked, span), 1)
        own_scores = jnp.where(column <= row, own_scores, MASKED)
        before_scores = scores_of(queries, before_ref[:block_len, :])
        before_scores = jnp.where(has_before, before_scores, MASKED)
        top = jnp.maximum(
            jnp.max(own_scores, axis=1, keepdims=True), jnp.max(before_scores, axis=1, keepdims=True)
        )
        sums = weigh(own_scores, top, own_ref[block_len : block_len + span, :])
        sums += weigh(before_scores, top, before_ref[block_len:, :])
        sums_ref[c * stacked : (c + 1) * stacked, :] = sums
        top_ref[c * stacked : (c + 1) * stacked, :] = jnp.broadcast_to(top, (stacked, HD))


def far_kernel(flag_ref, query_ref, got_ref, sums_ref, top_ref, out_ref):
    quarter, width = query_ref.shape
    pieces = got_ref.shape[0] // 2
    queries = stack_heads(query_ref[...])
    tops, parts = top_ref[...], []
    for r in range(2):
        scores = scores_of(queries, got_ref[:pieces, r].reshape(-1, HD))
        scores = jnp.where(flag_ref[r + 1] > 0, scores, MASKED)
        tops = jnp.maximum(tops, jnp.max(scores, axis=1, keepdims=True))
        parts.append(scores)
    top = tops[:, :1]
    sums = sums_ref[...] * jnp.exp2((top_ref[:, :1] - top) * (LOG2E * HD**-0.5))
    for r in range(2):
        sums += weigh(parts[r], top, got_ref[pieces:, r].reshape(-1, HD))
    done = (sums[:, :HD] / sums[:, HD:]).astype(jnp.bfloat16)
    for h in range(width // HD):
        out_ref[:, h * HD : (h + 1) * HD] = done[h * quarter : (h + 1) * quarter]


def attend_near(flags, queries, own, before):
    block_len, width = queries.shape
    stacked = block_len * width // HD
    return pl.pallas_call(
        near_kernel,
        out_shape=(
            jax.ShapeDtypeStruct((stacked, 2 * HD), jnp.float32),
            jax.ShapeDtypeStruct((stacked, HD), jnp.float32),
        ),
        in_specs=[pl.BlockSpec(memory_space=pltpu.SMEM)] + [pl.BlockSpec(memory_space=pltpu.VMEM)] * 3,
        out_specs=[pl.BlockSpec(memory_space=pltpu.VMEM)] * 2,
        compiler_params=pltpu.CompilerParams(vmem_limit_bytes=32 * 2**20),
        cost_estimate=pl.CostEstimate(
            flops=4 * stacked * block_len * HD * 2, bytes_accessed=2**22, transcendentals=2**21
        ),
        name="attend_near",
    )(flags, queries, own, before)


def attend_far(flags, queries, got, sums, top):
    block_len, width = queries.shape
    quarter = block_len // RING
    stacked = quarter * width // HD
    return pl.pallas_call(
        far_kernel,
        grid=(RING,),
        out_shape=jax.ShapeDtypeStruct((block_len, width), jnp.bfloat16),
        in_specs=[
            pl.BlockSpec(memory_space=pltpu.SMEM),
            pl.BlockSpec((quarter, width), lambda c: (c, 0)),
            pl.BlockSpec(got.shape, lambda c: (0, 0, 0, 0)),
            pl.BlockSpec((stacked, 2 * HD), lambda c: (c, 0)),
            pl.BlockSpec((stacked, HD), lambda c: (c, 0)),
        ],
        out_specs=pl.BlockSpec((quarter, width), lambda c: (c, 0)),
        compiler_params=pltpu.CompilerParams(vmem_limit_bytes=32 * 2**20),
        cost_estimate=pl.CostEstimate(
            flops=16 * stacked * block_len * HD * 2, bytes_accessed=2**22, transcendentals=2**22
        ),
        name="attend_far",
    )(flags, queries, got, sums, top)


RING = 4
RIGHT = [(i, (i + 1) % RING) for i in range(RING)]
LEFT = [(i, (i - 1) % RING) for i in range(RING)]
EVEN = [(i, i ^ 1) for i in range(RING)]
ODD = [(i, RING - 1 - i) for i in range(RING)]


def project_out(attended, w_out, w_near, me):
    rows, depth = attended.shape
    quarter, half = rows // RING, w_out.shape[1] // 2
    even, odd = me ^ 1, RING - 1 - me
    parts = attended.reshape(RING, quarter, depth)

    def pick(one, two):
        return jnp.concatenate(
            [
                lax.dynamic_index_in_dim(parts, one, 0, keepdims=False),
                lax.dynamic_index_in_dim(parts, two, 0, keepdims=False),
            ],
            axis=0,
        )

    across = (me + 2) % RING
    got_even = lax.ppermute(pick(even, across), "kvh", EVEN)
    got_odd = lax.ppermute(pick(odd, across), "kvh", ODD)

    def times(rows, w):
        return jnp.dot(rows, w, preferred_element_type=jnp.float32)

    sums_first = times(pick(me, odd), w_out[:, :half]) + times(got_even, w_near[:, :half])
    sums_second = times(pick(me, even), w_out[:, half:]) + times(got_odd, w_near[:, half:])
    other_first = lax.ppermute(sums_first[quarter:].astype(jnp.bfloat16), "kvh", ODD)
    other_second = lax.ppermute(sums_second[quarter:].astype(jnp.bfloat16), "kvh", EVEN)
    return jnp.concatenate(
        [
            (sums_first[:quarter] + other_first.astype(jnp.float32)).astype(jnp.bfloat16),
            (sums_second[:quarter] + other_second.astype(jnp.float32)).astype(jnp.bfloat16),
        ],
        axis=1,
    )


def local(tokens, norm_gain, w_query, w_key, w_value, w_out, picks):
    me, block_index = lax.axis_index("kvh"), lax.axis_index("ctx")
    ctx_count = lax.axis_size("ctx")
    block_len = tokens.shape[0]
    half = block_len // 2
    chosen = picks[0, 0]

    share = w_out.shape[0] // ctx_count
    passed = lax.dynamic_slice_in_dim(w_out, block_index * share, share, 0)
    mid = w_out.shape[1] // 2
    w_near = lax.all_gather(
        jnp.concatenate(
            [lax.ppermute(passed[:, :mid], "kvh", EVEN), lax.ppermute(passed[:, mid:], "kvh", ODD)],
            axis=1,
        ),
        "ctx",
        axis=0,
        tiled=True,
    )

    wanted = lax.all_to_all(
        jnp.broadcast_to(chosen[None, None, 1:], (ctx_count, 1, 2)), "ctx", 0, 0
    ).reshape(ctx_count * 2)

    width = tokens.shape[1]
    from_left = lax.ppermute(tokens, "kvh", RIGHT)
    from_right = lax.ppermute(tokens, "kvh", LEFT)
    upper = lax.ppermute(from_left[:half], "kvh", RIGHT)
    lower = lax.ppermute(from_right[half:], "kvh", LEFT)

    def weights(w, place):
        start = place % RING * width
        rows = lax.dynamic_slice_in_dim(w, start, width, 0)
        return (rows * lax.dynamic_slice_in_dim(norm_gain, start, width, 0)[:, None]).astype(jnp.bfloat16)

    def project(columns):
        own, left, right, across = (weights(columns, me + step) for step in (0, 3, 1, 2))

        def times(rows, w):
            return jnp.dot(rows, w, preferred_element_type=jnp.float32)

        sofar = times(tokens, own) + times(from_left, left) + times(from_right, right)
        return sofar + jnp.concatenate([times(upper, across), times(lower, across)], axis=0)

    def squares(rows):
        return jnp.sum(jnp.square(rows.astype(jnp.float32)), axis=1, keepdims=True)

    square_sum = squares(tokens) + squares(from_left) + squares(from_right)
    square_sum += jnp.concatenate([squares(upper), squares(lower)], axis=0)
    scale = lax.rsqrt(square_sum / (RING * width) + 1e-05)

    positions = block_index * block_len + jnp.arange(block_len, dtype=jnp.int32)
    kv = project(jnp.concatenate([w_key, w_value], axis=1)) * scale
    key_rows = rotate_pairs(kv[:, None, :HD], positions)[:, 0].astype(jnp.bfloat16)
    own = jnp.concatenate([key_rows, kv[:, HD:].astype(jnp.bfloat16)], axis=0)
    held = lax.all_to_all(own.reshape(ctx_count, -1, HD), "ctx", 0, 0)
    before = lax.ppermute(own, "ctx", [(i, i + 1) for i in range(ctx_count - 1)])
    got = lax.all_to_all(held[wanted].reshape(ctx_count, 2, -1, HD), "ctx", 0, 0)

    queries = (project(w_query) * scale).reshape(block_len, -1, HD)
    queries = rotate_pairs(queries, positions).astype(jnp.bfloat16).reshape(block_len, -1)
    flags = (chosen < block_index).astype(jnp.int32)
    sums, top = attend_near(flags, queries, own, before)
    attended = attend_far(flags, queries, got, sums, top)
    return project_out(attended, w_out, w_near, me)


def solution(mesh):
    in_specs = (
        P("ctx", "kvh"),
        P(),
        P(None, "kvh"),
        P(None, "kvh"),
        P(None, "kvh"),
        P("kvh", None),
        P("ctx", "kvh", None),
    )
    out_specs = P(("ctx", "kvh"), None)
    return jax.shard_map(local, mesh=mesh, in_specs=in_specs, out_specs=out_specs, check_vma=False)
```

```python
import jax
import jax.numpy as jnp
from jax import lax
from jax.experimental import pallas as pl
from jax.experimental.pallas import tpu as pltpu
from jax.sharding import PartitionSpec as P

HD = 128


ROPE_BASE = 500000.0


def rotate_pairs(head_rows, positions):
    half_dim = head_rows.shape[-1] // 2
    frequency = ROPE_BASE ** (-jnp.arange(half_dim, dtype=jnp.float32) * 2.0 / head_rows.shape[-1])
    angles = positions.astype(jnp.float32)[:, None] * frequency[None, :]
    cosine = jnp.cos(angles)[:, None, :]
    sine_part = jnp.sin(angles)[:, None, :]
    lower_half = head_rows[..., :half_dim]
    upper_half = head_rows[..., half_dim:]
    return jnp.concatenate(
        [
            lower_half * cosine - upper_half * sine_part,
            upper_half * cosine + lower_half * sine_part,
        ],
        axis=-1,
    )


SCALE = 1.4426950408889634 * HD**-0.5
MASKED = -1e30


def stack_heads(rows):
    return jnp.concatenate(
        [rows[:, h * HD : (h + 1) * HD] for h in range(rows.shape[1] // HD)], axis=0
    )


def scores_of(queries, keys):
    return lax.dot_general(
        queries, keys, (((1,), (1,)), ((), ())), preferred_element_type=jnp.float32
    )


def weigh(scores, offset, values):
    weights = jnp.exp2(scores * SCALE - offset).astype(jnp.bfloat16)
    wide = jnp.concatenate([values, jnp.ones_like(values)], axis=1)
    return jnp.dot(weights, wide, preferred_element_type=jnp.float32)


def row_max(scores):
    return jnp.max(scores, axis=1, keepdims=True)


def near_kernel(flag_ref, query_ref, own_ref, before_ref, sums_ref, stats_ref):
    block_len = query_ref.shape[0]
    quarter = block_len // RING
    heads = query_ref.shape[1] // HD
    stacked = quarter * heads
    has_before = flag_ref[0] > 0
    hidden = jnp.where(has_before, 0.0, -MASKED)
    row = lax.broadcasted_iota(jnp.int32, (stacked, quarter), 0) % quarter
    causal = lax.broadcasted_iota(jnp.int32, (stacked, quarter), 1) <= row
    left = lax.broadcasted_iota(jnp.int32, (stacked, HD), 1) < HD // 2
    for c in range(RING):
        start, end = c * quarter, (c + 1) * quarter
        queries = stack_heads(query_ref[start:end, :])
        own_scores = jnp.where(causal, scores_of(queries, own_ref[start:end, :]), MASKED)
        before_scores = scores_of(queries, before_ref[:block_len, :])
        top = jnp.maximum(
            row_max(own_scores), jnp.where(has_before, row_max(before_scores), MASKED)
        )
        if c:
            early_scores = scores_of(queries, own_ref[:start, :])
            top = jnp.maximum(top, row_max(early_scores))
        offset = top * SCALE
        sums = weigh(own_scores, offset, own_ref[block_len + start : block_len + end, :])
        sums += weigh(before_scores, offset + hidden, before_ref[block_len:, :])
        if c:
            sums += weigh(early_scores, offset, own_ref[block_len : block_len + start, :])
        rows = slice(c * stacked, (c + 1) * stacked)
        sums_ref[rows, :] = sums[:, :HD]
        stats_ref[rows, :] = jnp.where(left, sums[:, HD:], top)


def far_kernel(flag_ref, query_ref, got_ref, sums_ref, stats_ref, out_ref):
    block_len, width = query_ref.shape
    quarter = block_len // RING
    heads = width // HD
    stacked = quarter * heads
    pieces = got_ref.shape[0] // 2
    for c in range(RING):
        rows = slice(c * stacked, (c + 1) * stacked)
        queries = stack_heads(query_ref[c * quarter : (c + 1) * quarter, :])
        before_top = stats_ref[rows, HD // 2 : HD // 2 + 1]
        top, parts = before_top, []
        for r in range(2):
            scores = scores_of(queries, got_ref[:pieces, r].reshape(-1, HD))
            top = jnp.maximum(top, jnp.where(flag_ref[r + 1] > 0, row_max(scores), MASKED))
            parts.append(scores)
        offset = top * SCALE
        shrink = jnp.exp2((before_top - top) * SCALE)
        total = stats_ref[rows, :1] * shrink
        sums = sums_ref[rows, :] * shrink
        for r in range(2):
            hidden = jnp.where(flag_ref[r + 1] > 0, 0.0, -MASKED)
            more = weigh(parts[r], offset + hidden, got_ref[pieces:, r].reshape(-1, HD))
            sums += more[:, :HD]
            total += more[:, HD:]
        done = (sums / total).astype(jnp.bfloat16)
        for h in range(heads):
            out_ref[c * quarter : (c + 1) * quarter, h * HD : (h + 1) * HD] = done[
                h * quarter : (h + 1) * quarter
            ]


def route_kernel(wanted_ref, held_ref, out_ref):
    for i in range(out_ref.shape[0]):
        out_ref[i] = held_ref[wanted_ref[i]]


VMEM = pl.BlockSpec(memory_space=pltpu.VMEM)
SMEM = pl.BlockSpec(memory_space=pltpu.SMEM)


def call(kernel, out_shape, operands, flops, name):
    return pl.pallas_call(
        kernel,
        out_shape=out_shape,
        in_specs=[SMEM] + [VMEM] * (len(operands) - 1),
        out_specs=[VMEM] * len(out_shape),
        compiler_params=pltpu.CompilerParams(vmem_limit_bytes=40 * 2**20),
        cost_estimate=pl.CostEstimate(flops=flops, bytes_accessed=2**22, transcendentals=2**21),
        name=name,
    )(*operands)


def attend_near(flags, queries, own, before):
    block_len, width = queries.shape
    stacked = block_len * width // HD
    shape = jax.ShapeDtypeStruct((stacked, HD), jnp.float32)
    flops = 8 * stacked * block_len * HD
    return call(near_kernel, [shape, shape], (flags, queries, own, before), flops, "attend_near")


def attend_far(flags, queries, got, sums, stats):
    block_len, width = queries.shape
    shape = jax.ShapeDtypeStruct((block_len, width), jnp.bfloat16)
    flops = 8 * block_len * width * block_len
    return call(far_kernel, [shape], (flags, queries, got, sums, stats), flops, "attend_far")[0]


def route(wanted, held):
    shape = jax.ShapeDtypeStruct(wanted.shape + held.shape[1:], held.dtype)
    return call(route_kernel, [shape], (wanted, held), 2**20, "route")[0]


RING = 4
RIGHT = [(i, (i + 1) % RING) for i in range(RING)]
LEFT = [(i, (i - 1) % RING) for i in range(RING)]
EVEN = [(i, i ^ 1) for i in range(RING)]
ODD = [(i, RING - 1 - i) for i in range(RING)]


def project_out(attended, w_out, w_near, me):
    rows, depth = attended.shape
    quarter, half = rows // RING, w_out.shape[1] // 2
    even, odd = me ^ 1, RING - 1 - me
    parts = attended.reshape(RING, quarter, depth)

    def pick(one, two):
        return jnp.concatenate(
            [
                lax.dynamic_index_in_dim(parts, one, 0, keepdims=False),
                lax.dynamic_index_in_dim(parts, two, 0, keepdims=False),
            ],
            axis=0,
        )

    across = (me + 2) % RING
    got_even = lax.ppermute(pick(even, across), "kvh", EVEN)
    got_odd = lax.ppermute(pick(odd, across), "kvh", ODD)

    def times(rows, w):
        return jnp.dot(rows, w, preferred_element_type=jnp.float32)

    def part(index):
        return lax.dynamic_index_in_dim(parts, index, 0, keepdims=False)

    sent_first = times(part(odd), w_out[:, :half]) + times(got_even[quarter:], w_near[:, :half])
    sent_second = times(part(even), w_out[:, half:]) + times(got_odd[quarter:], w_near[:, half:])
    other_first = lax.ppermute(sent_first.astype(jnp.bfloat16), "kvh", ODD)
    other_second = lax.ppermute(sent_second.astype(jnp.bfloat16), "kvh", EVEN)
    kept = times(part(me), w_out)
    kept_first = kept[:, :half] + times(got_even[:quarter], w_near[:, :half])
    kept_second = kept[:, half:] + times(got_odd[:quarter], w_near[:, half:])
    return jnp.concatenate(
        [
            (kept_first + other_first.astype(jnp.float32)).astype(jnp.bfloat16),
            (kept_second + other_second.astype(jnp.float32)).astype(jnp.bfloat16),
        ],
        axis=1,
    )


SIZES = (8, 4, 2)


def shift(axis, step):
    _, ys, cs = SIZES
    strides = (ys * cs, cs, 1)
    pairs = []
    for i in range(SIZES[0] * ys * cs):
        place = i // strides[axis] % SIZES[axis]
        source = i + ((place + step) % SIZES[axis] - place) * strides[axis]
        pairs.append((source, i))
    return pairs


def gather_near(passed, block_index):
    share, width = passed.shape
    mid = width // 2
    piece = jnp.concatenate(
        [lax.ppermute(passed[:, :mid], "kvh", EVEN), lax.ppermute(passed[:, mid:], "kvh", ODD)],
        axis=1,
    )

    def fetch(rows, axis, step):
        return lax.ppermute(rows, "ctx", shift(axis, step))

    trio = jnp.concatenate([fetch(piece, 0, -1), piece, fetch(piece, 0, 1)], axis=0)
    along_z = jnp.concatenate([trio, fetch(trio, 0, 3), fetch(trio[share:], 0, -3)], axis=0)
    plane = jnp.concatenate(
        [along_z, fetch(along_z, 1, -1), fetch(along_z, 1, 1), fetch(along_z, 1, 2)], axis=0
    )
    whole = jnp.concatenate([plane, fetch(plane, 2, 1)], axis=0)
    zs, ys, cs = SIZES
    z, y, c = block_index // (ys * cs), block_index // cs % ys, block_index % cs
    z_of = (z + jnp.array([-1, 0, 1, 2, 3, 4, -3, -2])) % zs
    y_of = (y + jnp.array([0, -1, 1, 2])) % ys
    c_of = (c + jnp.array([0, 1])) % cs
    place = ((z_of[None, None, :] * ys + y_of[None, :, None]) * cs + c_of[:, None, None]).reshape(-1)
    place = (place[:, None] * share + jnp.arange(share)).reshape(-1)
    turn = (jnp.arange(place.size)[:, None] == place[None, :]).astype(whole.dtype)
    return jnp.dot(turn, whole, preferred_element_type=jnp.float32).astype(whole.dtype)


def local(tokens, norm_gain, w_query, w_key, w_value, w_out, picks):
    me, block_index = lax.axis_index("kvh"), lax.axis_index("ctx")
    ctx_count = lax.axis_size("ctx")
    block_len = tokens.shape[0]
    half = block_len // 2
    chosen = picks[0, 0]

    wanted = lax.all_to_all(
        jnp.broadcast_to(chosen[None, None, 1:], (ctx_count, 1, 2)), "ctx", 0, 0
    ).reshape(ctx_count * 2)

    width = tokens.shape[1]
    from_left = lax.ppermute(tokens, "kvh", RIGHT)
    from_right = lax.ppermute(tokens, "kvh", LEFT)
    share = w_out.shape[0] // ctx_count
    passed = lax.dynamic_slice_in_dim(w_out, block_index * share, share, 0)
    passed, _ = lax.optimization_barrier((passed, from_left))
    w_near = gather_near(passed, block_index)
    upper = lax.ppermute(from_left[:half], "kvh", RIGHT)
    lower = lax.ppermute(from_right[half:], "kvh", LEFT)

    def weights(w, place):
        start = place % RING * width
        rows = lax.dynamic_slice_in_dim(w, start, width, 0)
        return (rows * lax.dynamic_slice_in_dim(norm_gain, start, width, 0)[:, None]).astype(jnp.bfloat16)

    def project(columns):
        own, left, right, across = (weights(columns, me + step) for step in (0, 3, 1, 2))

        def times(rows, w):
            return jnp.dot(rows, w, preferred_element_type=jnp.float32)

        sofar = times(tokens, own) + times(from_left, left) + times(from_right, right)
        return sofar + jnp.concatenate([times(upper, across), times(lower, across)], axis=0)

    def squares(rows):
        return jnp.sum(jnp.square(rows.astype(jnp.float32)), axis=1, keepdims=True)

    square_sum = squares(tokens) + squares(from_left) + squares(from_right)
    square_sum += jnp.concatenate([squares(upper), squares(lower)], axis=0)
    scale = lax.rsqrt(square_sum / (RING * width) + 1e-05)

    positions = block_index * block_len + jnp.arange(block_len, dtype=jnp.int32)
    kv = project(jnp.concatenate([w_key, w_value], axis=1)) * scale
    key_rows = rotate_pairs(kv[:, None, :HD], positions)[:, 0].astype(jnp.bfloat16)
    own = jnp.concatenate([key_rows, kv[:, HD:].astype(jnp.bfloat16)], axis=0)
    held = lax.all_to_all(own.reshape(ctx_count, -1, HD), "ctx", 0, 0)
    before = lax.ppermute(own, "ctx", [(i, i + 1) for i in range(ctx_count - 1)])
    got = lax.all_to_all(route(wanted, held).reshape(ctx_count, 2, -1, HD), "ctx", 0, 0)

    queries = (project(w_query) * scale).reshape(block_len, -1, HD)
    queries = rotate_pairs(queries, positions).astype(jnp.bfloat16).reshape(block_len, -1)
    flags = (chosen < block_index).astype(jnp.int32)
    sums, stats = attend_near(flags, queries, own, before)
    attended = attend_far(flags, queries, got, sums, stats)
    return project_out(attended, w_out, w_near, me)


def solution(mesh):
    in_specs = (
        P("ctx", "kvh"),
        P(),
        P(None, "kvh"),
        P(None, "kvh"),
        P(None, "kvh"),
        P("kvh", None),
        P("ctx", "kvh", None),
    )
    out_specs = P(("ctx", "kvh"), None)
    return jax.shard_map(local, mesh=mesh, in_specs=in_specs, out_specs=out_specs, check_vma=False)
```

```python
import jax
import jax.numpy as jnp
from jax import lax
from jax.experimental import pallas as pl
from jax.experimental.pallas import tpu as pltpu
from jax.sharding import PartitionSpec as P

HD = 128


ROPE_BASE = 500000.0


def rotate_pairs(head_rows, positions):
    half_dim = head_rows.shape[-1] // 2
    frequency = ROPE_BASE ** (-jnp.arange(half_dim, dtype=jnp.float32) * 2.0 / head_rows.shape[-1])
    angles = positions.astype(jnp.float32)[:, None] * frequency[None, :]
    cosine = jnp.cos(angles)[:, None, :]
    sine_part = jnp.sin(angles)[:, None, :]
    lower_half = head_rows[..., :half_dim]
    upper_half = head_rows[..., half_dim:]
    return jnp.concatenate(
        [
            lower_half * cosine - upper_half * sine_part,
            upper_half * cosine + lower_half * sine_part,
        ],
        axis=-1,
    )


SCALE = 1.4426950408889634 * HD**-0.5
MASKED = -1e30


def stack_heads(rows):
    return jnp.concatenate(
        [rows[:, h * HD : (h + 1) * HD] for h in range(rows.shape[1] // HD)], axis=0
    )


def scores_of(queries, keys):
    return lax.dot_general(
        queries, keys, (((1,), (1,)), ((), ())), preferred_element_type=jnp.float32
    )


def weigh(scores, offset, values):
    weights = jnp.exp2(scores * SCALE - offset).astype(jnp.bfloat16)
    wide = jnp.concatenate([values, jnp.ones_like(values)], axis=1)
    return jnp.dot(weights, wide, preferred_element_type=jnp.float32)


def row_max(scores):
    return jnp.max(scores, axis=1, keepdims=True)


def near_kernel(flag_ref, query_ref, own_ref, before_ref, sums_ref, stats_ref):
    block_len = query_ref.shape[0]
    quarter = block_len // RING
    heads = query_ref.shape[1] // HD
    stacked = quarter * heads
    has_before = flag_ref[0] > 0
    hidden = jnp.where(has_before, 0.0, -MASKED)
    row = lax.broadcasted_iota(jnp.int32, (stacked, quarter), 0) % quarter
    causal = lax.broadcasted_iota(jnp.int32, (stacked, quarter), 1) <= row
    left = lax.broadcasted_iota(jnp.int32, (stacked, HD), 1) < HD // 2
    for c in range(RING):
        start, end = c * quarter, (c + 1) * quarter
        queries = stack_heads(query_ref[start:end, :])
        own_scores = jnp.where(causal, scores_of(queries, own_ref[start:end, :]), MASKED)
        before_scores = scores_of(queries, before_ref[:block_len, :])
        top = jnp.maximum(
            row_max(own_scores), jnp.where(has_before, row_max(before_scores), MASKED)
        )
        if c:
            early_scores = scores_of(queries, own_ref[:start, :])
            top = jnp.maximum(top, row_max(early_scores))
        offset = top * SCALE
        sums = weigh(own_scores, offset, own_ref[block_len + start : block_len + end, :])
        sums += weigh(before_scores, offset + hidden, before_ref[block_len:, :])
        if c:
            sums += weigh(early_scores, offset, own_ref[block_len : block_len + start, :])
        rows = slice(c * stacked, (c + 1) * stacked)
        sums_ref[rows, :] = sums[:, :HD]
        stats_ref[rows, :] = jnp.where(left, sums[:, HD:], top)


def far_kernel(flag_ref, query_ref, got_ref, sums_ref, stats_ref, out_ref):
    block_len, width = query_ref.shape
    quarter = block_len // RING
    heads = width // HD
    stacked = quarter * heads
    pieces = got_ref.shape[0] // 2
    for c in range(RING):
        rows = slice(c * stacked, (c + 1) * stacked)
        queries = stack_heads(query_ref[c * quarter : (c + 1) * quarter, :])
        before_top = stats_ref[rows, HD // 2 : HD // 2 + 1]
        top, parts = before_top, []
        for r in range(2):
            scores = scores_of(queries, got_ref[:pieces, r].reshape(-1, HD))
            top = jnp.maximum(top, jnp.where(flag_ref[r + 1] > 0, row_max(scores), MASKED))
            parts.append(scores)
        offset = top * SCALE
        shrink = jnp.exp2((before_top - top) * SCALE)
        total = stats_ref[rows, :1] * shrink
        sums = sums_ref[rows, :] * shrink
        for r in range(2):
            hidden = jnp.where(flag_ref[r + 1] > 0, 0.0, -MASKED)
            more = weigh(parts[r], offset + hidden, got_ref[pieces:, r].reshape(-1, HD))
            sums += more[:, :HD]
            total += more[:, HD:]
        done = (sums / total).astype(jnp.bfloat16)
        for h in range(heads):
            out_ref[c * quarter : (c + 1) * quarter, h * HD : (h + 1) * HD] = done[
                h * quarter : (h + 1) * quarter
            ]


def route_kernel(wanted_ref, held_ref, out_ref):
    for i in range(out_ref.shape[0]):
        out_ref[i] = held_ref[wanted_ref[i]]


VMEM = pl.BlockSpec(memory_space=pltpu.VMEM)
SMEM = pl.BlockSpec(memory_space=pltpu.SMEM)


def call(kernel, out_shape, operands, flops, name):
    return pl.pallas_call(
        kernel,
        out_shape=out_shape,
        in_specs=[SMEM] + [VMEM] * (len(operands) - 1),
        out_specs=[VMEM] * len(out_shape),
        compiler_params=pltpu.CompilerParams(vmem_limit_bytes=40 * 2**20),
        cost_estimate=pl.CostEstimate(flops=flops, bytes_accessed=2**22, transcendentals=2**21),
        name=name,
    )(*operands)


def attend_near(flags, queries, own, before):
    block_len, width = queries.shape
    stacked = block_len * width // HD
    shape = jax.ShapeDtypeStruct((stacked, HD), jnp.float32)
    flops = 8 * stacked * block_len * HD
    return call(near_kernel, [shape, shape], (flags, queries, own, before), flops, "attend_near")


def attend_far(flags, queries, got, sums, stats):
    block_len, width = queries.shape
    shape = jax.ShapeDtypeStruct((block_len, width), jnp.bfloat16)
    flops = 8 * block_len * width * block_len
    return call(far_kernel, [shape], (flags, queries, got, sums, stats), flops, "attend_far")[0]


def route(wanted, held):
    shape = jax.ShapeDtypeStruct(wanted.shape + held.shape[1:], held.dtype)
    return call(route_kernel, [shape], (wanted, held), 2**20, "route")[0]


RING = 4
RIGHT = [(i, (i + 1) % RING) for i in range(RING)]
LEFT = [(i, (i - 1) % RING) for i in range(RING)]
EVEN = [(i, i ^ 1) for i in range(RING)]
ODD = [(i, RING - 1 - i) for i in range(RING)]


def project_out(attended, w_out, w_near, me):
    rows, depth = attended.shape
    quarter, half = rows // RING, w_out.shape[1] // 2
    even, odd = me ^ 1, RING - 1 - me
    parts = attended.reshape(RING, quarter, depth)

    def pick(one, two):
        return jnp.concatenate(
            [
                lax.dynamic_index_in_dim(parts, one, 0, keepdims=False),
                lax.dynamic_index_in_dim(parts, two, 0, keepdims=False),
            ],
            axis=0,
        )

    across = (me + 2) % RING
    got_even = lax.ppermute(pick(even, across), "kvh", EVEN)
    got_odd = lax.ppermute(pick(odd, across), "kvh", ODD)

    def times(rows, w):
        return jnp.dot(rows, w, preferred_element_type=jnp.float32)

    def part(index):
        return lax.dynamic_index_in_dim(parts, index, 0, keepdims=False)

    sent_first = times(part(odd), w_out[:, :half]) + times(got_even[quarter:], w_near[:, :half])
    sent_second = times(part(even), w_out[:, half:]) + times(got_odd[quarter:], w_near[:, half:])
    other_first = lax.ppermute(sent_first.astype(jnp.bfloat16), "kvh", ODD)
    other_second = lax.ppermute(sent_second.astype(jnp.bfloat16), "kvh", EVEN)
    kept = times(part(me), w_out)
    kept_first = kept[:, :half] + times(got_even[:quarter], w_near[:, :half])
    kept_second = kept[:, half:] + times(got_odd[:quarter], w_near[:, half:])
    return jnp.concatenate(
        [
            (kept_first + other_first.astype(jnp.float32)).astype(jnp.bfloat16),
            (kept_second + other_second.astype(jnp.float32)).astype(jnp.bfloat16),
        ],
        axis=1,
    )


SIZES = (8, 4, 2)


def shift(axis, step):
    _, ys, cs = SIZES
    strides = (ys * cs, cs, 1)
    pairs = []
    for i in range(SIZES[0] * ys * cs):
        place = i // strides[axis] % SIZES[axis]
        source = i + ((place + step) % SIZES[axis] - place) * strides[axis]
        pairs.append((source, i))
    return pairs


def after(value, *others):
    return lax.optimization_barrier((value, *others))[0]


def gather_near(passed, block_index, first, second, third):
    share, width = passed.shape
    passed = after(passed, first)
    mid = width // 2
    piece = jnp.concatenate(
        [lax.ppermute(passed[:, :mid], "kvh", EVEN), lax.ppermute(passed[:, mid:], "kvh", ODD)],
        axis=1,
    )

    def fetch(rows, axis, step):
        return lax.ppermute(rows, "ctx", shift(axis, step))

    trio = jnp.concatenate([fetch(piece, 0, -1), piece, fetch(piece, 0, 1)], axis=0)
    along_z = jnp.concatenate([trio, fetch(trio, 0, 3), fetch(trio[share:], 0, -3)], axis=0)
    along_z = after(along_z, second)
    plane = jnp.concatenate(
        [along_z, fetch(along_z, 1, -1), fetch(along_z, 1, 1), fetch(along_z, 1, 2)], axis=0
    )
    plane = after(plane, third)
    whole = jnp.concatenate([plane, fetch(plane, 2, 1)], axis=0)
    zs, ys, cs = SIZES
    z, y, c = block_index // (ys * cs), block_index // cs % ys, block_index % cs
    z_of = (z + jnp.array([-1, 0, 1, 2, 3, 4, -3, -2])) % zs
    y_of = (y + jnp.array([0, -1, 1, 2])) % ys
    c_of = (c + jnp.array([0, 1])) % cs
    place = ((z_of[None, None, :] * ys + y_of[None, :, None]) * cs + c_of[:, None, None]).reshape(-1)
    place = (place[:, None] * share + jnp.arange(share)).reshape(-1)
    turn = (jnp.arange(place.size)[:, None] == place[None, :]).astype(whole.dtype)
    return jnp.dot(turn, whole, preferred_element_type=jnp.float32).astype(whole.dtype)


def local(tokens, norm_gain, w_query, w_key, w_value, w_out, picks):
    me, block_index = lax.axis_index("kvh"), lax.axis_index("ctx")
    ctx_count = lax.axis_size("ctx")
    block_len = tokens.shape[0]
    half = block_len // 2
    chosen = picks[0, 0]

    wanted = lax.all_to_all(
        jnp.broadcast_to(chosen[None, None, 1:], (ctx_count, 1, 2)), "ctx", 0, 0
    ).reshape(ctx_count * 2)

    width = tokens.shape[1]
    from_left = lax.ppermute(tokens, "kvh", RIGHT)
    from_right = lax.ppermute(tokens, "kvh", LEFT)
    upper = lax.ppermute(from_left[:half], "kvh", RIGHT)
    lower = lax.ppermute(from_right[half:], "kvh", LEFT)

    def weights(w, place):
        start = place % RING * width
        rows = lax.dynamic_slice_in_dim(w, start, width, 0)
        return (rows * lax.dynamic_slice_in_dim(norm_gain, start, width, 0)[:, None]).astype(jnp.bfloat16)

    def project(columns):
        own, left, right, across = (weights(columns, me + step) for step in (0, 3, 1, 2))

        def times(rows, w):
            return jnp.dot(rows, w, preferred_element_type=jnp.float32)

        sofar = times(tokens, own) + times(from_left, left) + times(from_right, right)
        return sofar, sofar + jnp.concatenate([times(upper, across), times(lower, across)], axis=0)

    def squares(rows):
        return jnp.sum(jnp.square(rows.astype(jnp.float32)), axis=1, keepdims=True)

    square_sum = squares(tokens) + squares(from_left) + squares(from_right)
    square_sum += jnp.concatenate([squares(upper), squares(lower)], axis=0)
    scale = lax.rsqrt(square_sum / (RING * width) + 1e-05)

    positions = block_index * block_len + jnp.arange(block_len, dtype=jnp.int32)
    sofar, kv = project(jnp.concatenate([w_key, w_value], axis=1))
    kv = kv * scale
    key_rows = rotate_pairs(kv[:, None, :HD], positions)[:, 0].astype(jnp.bfloat16)
    own = jnp.concatenate([key_rows, kv[:, HD:].astype(jnp.bfloat16)], axis=0)
    held = lax.all_to_all(own.reshape(ctx_count, -1, HD), "ctx", 0, 0)
    before = lax.ppermute(own, "ctx", [(i, i + 1) for i in range(ctx_count - 1)])
    got = lax.all_to_all(route(wanted, held).reshape(ctx_count, 2, -1, HD), "ctx", 0, 0)

    share = w_out.shape[0] // ctx_count
    passed = lax.dynamic_slice_in_dim(w_out, block_index * share, share, 0)
    w_near = gather_near(passed, block_index, sofar, own, held)

    queries = (project(after(w_query, own))[1] * scale).reshape(block_len, -1, HD)
    queries = rotate_pairs(queries, positions).astype(jnp.bfloat16).reshape(block_len, -1)
    flags = (chosen < block_index).astype(jnp.int32)
    sums, stats = attend_near(flags, queries, own, before)
    attended = attend_far(flags, queries, got, sums, stats)
    return project_out(attended, w_out, w_near, me)


def solution(mesh):
    in_specs = (
        P("ctx", "kvh"),
        P(),
        P(None, "kvh"),
        P(None, "kvh"),
        P(None, "kvh"),
        P("kvh", None),
        P("ctx", "kvh", None),
    )
    out_specs = P(("ctx", "kvh"), None)
    return jax.shard_map(local, mesh=mesh, in_specs=in_specs, out_specs=out_specs, check_vma=False)
```

```python
import jax
import jax.numpy as jnp
from jax import lax
from jax.experimental import pallas as pl
from jax.experimental.pallas import tpu as pltpu
from jax.sharding import PartitionSpec as P

HD = 128


ROPE_BASE = 500000.0


def rotate_pairs(head_rows, positions):
    half_dim = head_rows.shape[-1] // 2
    frequency = ROPE_BASE ** (-jnp.arange(half_dim, dtype=jnp.float32) * 2.0 / head_rows.shape[-1])
    angles = positions.astype(jnp.float32)[:, None] * frequency[None, :]
    cosine = jnp.cos(angles)[:, None, :]
    sine_part = jnp.sin(angles)[:, None, :]
    lower_half = head_rows[..., :half_dim]
    upper_half = head_rows[..., half_dim:]
    return jnp.concatenate(
        [
            lower_half * cosine - upper_half * sine_part,
            upper_half * cosine + lower_half * sine_part,
        ],
        axis=-1,
    )


SCALE = 1.4426950408889634 * HD**-0.5
MASKED = -1e30


def stack_heads(rows):
    return jnp.concatenate(
        [rows[:, h * HD : (h + 1) * HD] for h in range(rows.shape[1] // HD)], axis=0
    )


def scores_of(queries, keys):
    return lax.dot_general(
        queries, keys, (((1,), (1,)), ((), ())), preferred_element_type=jnp.float32
    )


def weigh(scores, offset, values):
    weights = jnp.exp2(scores * SCALE - offset).astype(jnp.bfloat16)
    wide = jnp.concatenate([values, jnp.ones_like(values)], axis=1)
    return jnp.dot(weights, wide, preferred_element_type=jnp.float32)


def row_max(scores):
    return jnp.max(scores, axis=1, keepdims=True)


def near_kernel(flag_ref, query_ref, own_ref, before_ref, sums_ref, stats_ref):
    block_len = query_ref.shape[0]
    quarter = block_len // RING
    heads = query_ref.shape[1] // HD
    stacked = quarter * heads
    has_before = flag_ref[0] > 0
    hidden = jnp.where(has_before, 0.0, -MASKED)
    row = lax.broadcasted_iota(jnp.int32, (stacked, quarter), 0) % quarter
    causal = lax.broadcasted_iota(jnp.int32, (stacked, quarter), 1) <= row
    left = lax.broadcasted_iota(jnp.int32, (stacked, HD), 1) < HD // 2
    for c in range(RING):
        start, end = c * quarter, (c + 1) * quarter
        queries = stack_heads(query_ref[start:end, :])
        own_scores = jnp.where(causal, scores_of(queries, own_ref[start:end, :]), MASKED)
        before_scores = scores_of(queries, before_ref[:block_len, :])
        top = jnp.maximum(
            row_max(own_scores), jnp.where(has_before, row_max(before_scores), MASKED)
        )
        if c:
            early_scores = scores_of(queries, own_ref[:start, :])
            top = jnp.maximum(top, row_max(early_scores))
        offset = top * SCALE
        sums = weigh(own_scores, offset, own_ref[block_len + start : block_len + end, :])
        sums += weigh(before_scores, offset + hidden, before_ref[block_len:, :])
        if c:
            sums += weigh(early_scores, offset, own_ref[block_len : block_len + start, :])
        rows = slice(c * stacked, (c + 1) * stacked)
        sums_ref[rows, :] = sums[:, :HD]
        stats_ref[rows, :] = jnp.where(left, sums[:, HD:], top)


def far_kernel(flag_ref, query_ref, got_ref, sums_ref, stats_ref, out_ref):
    block_len, width = query_ref.shape
    quarter = block_len // RING
    heads = width // HD
    stacked = quarter * heads
    pieces = got_ref.shape[0] // 2
    for c in range(RING):
        rows = slice(c * stacked, (c + 1) * stacked)
        queries = stack_heads(query_ref[c * quarter : (c + 1) * quarter, :])
        before_top = stats_ref[rows, HD // 2 : HD // 2 + 1]
        top, parts = before_top, []
        for r in range(2):
            scores = scores_of(queries, got_ref[:pieces, r].reshape(-1, HD))
            top = jnp.maximum(top, jnp.where(flag_ref[r + 1] > 0, row_max(scores), MASKED))
            parts.append(scores)
        offset = top * SCALE
        shrink = jnp.exp2((before_top - top) * SCALE)
        total = stats_ref[rows, :1] * shrink
        sums = sums_ref[rows, :] * shrink
        for r in range(2):
            hidden = jnp.where(flag_ref[r + 1] > 0, 0.0, -MASKED)
            more = weigh(parts[r], offset + hidden, got_ref[pieces:, r].reshape(-1, HD))
            sums += more[:, :HD]
            total += more[:, HD:]
        done = (sums / total).astype(jnp.bfloat16)
        for h in range(heads):
            out_ref[c * quarter : (c + 1) * quarter, h * HD : (h + 1) * HD] = done[
                h * quarter : (h + 1) * quarter
            ]


def route_kernel(wanted_ref, held_ref, out_ref):
    for i in range(out_ref.shape[0]):
        out_ref[i] = held_ref[wanted_ref[i]]


VMEM = pl.BlockSpec(memory_space=pltpu.VMEM)
SMEM = pl.BlockSpec(memory_space=pltpu.SMEM)


def call(kernel, out_shape, operands, flops, name):
    return pl.pallas_call(
        kernel,
        out_shape=out_shape,
        in_specs=[SMEM] + [VMEM] * (len(operands) - 1),
        out_specs=[VMEM] * len(out_shape),
        compiler_params=pltpu.CompilerParams(vmem_limit_bytes=40 * 2**20),
        cost_estimate=pl.CostEstimate(flops=flops, bytes_accessed=2**22, transcendentals=2**21),
        name=name,
    )(*operands)


def attend_near(flags, queries, own, before):
    block_len, width = queries.shape
    stacked = block_len * width // HD
    shape = jax.ShapeDtypeStruct((stacked, HD), jnp.float32)
    flops = 8 * stacked * block_len * HD
    return call(near_kernel, [shape, shape], (flags, queries, own, before), flops, "attend_near")


def attend_far(flags, queries, got, sums, stats):
    block_len, width = queries.shape
    shape = jax.ShapeDtypeStruct((block_len, width), jnp.bfloat16)
    flops = 8 * block_len * width * block_len
    return call(far_kernel, [shape], (flags, queries, got, sums, stats), flops, "attend_far")[0]


def route(wanted, held):
    shape = jax.ShapeDtypeStruct(wanted.shape + held.shape[1:], held.dtype)
    return call(route_kernel, [shape], (wanted, held), 2**20, "route")[0]


RING = 4
RIGHT = [(i, (i + 1) % RING) for i in range(RING)]
LEFT = [(i, (i - 1) % RING) for i in range(RING)]
EVEN = [(i, i ^ 1) for i in range(RING)]
ODD = [(i, RING - 1 - i) for i in range(RING)]


def project_out(attended, w_out, w_near, me):
    rows, depth = attended.shape
    quarter, half = rows // RING, w_out.shape[1] // 2
    even, odd = me ^ 1, RING - 1 - me
    parts = attended.reshape(RING, quarter, depth)

    def pick(one, two):
        return jnp.concatenate(
            [
                lax.dynamic_index_in_dim(parts, one, 0, keepdims=False),
                lax.dynamic_index_in_dim(parts, two, 0, keepdims=False),
            ],
            axis=0,
        )

    across = (me + 2) % RING
    got_even = lax.ppermute(pick(even, across), "kvh", EVEN)
    got_odd = lax.ppermute(pick(odd, across), "kvh", ODD)

    def times(rows, w):
        return jnp.dot(rows, w, preferred_element_type=jnp.float32)

    def part(index):
        return lax.dynamic_index_in_dim(parts, index, 0, keepdims=False)

    sent_first = times(part(odd), w_out[:, :half]) + times(got_even[quarter:], w_near[:, :half])
    sent_second = times(part(even), w_out[:, half:]) + times(got_odd[quarter:], w_near[:, half:])
    other_first = lax.ppermute(sent_first.astype(jnp.bfloat16), "kvh", ODD)
    other_second = lax.ppermute(sent_second.astype(jnp.bfloat16), "kvh", EVEN)
    kept = times(part(me), w_out)
    kept_first = kept[:, :half] + times(got_even[:quarter], w_near[:, :half])
    kept_second = kept[:, half:] + times(got_odd[:quarter], w_near[:, half:])
    return jnp.concatenate(
        [
            (kept_first + other_first.astype(jnp.float32)).astype(jnp.bfloat16),
            (kept_second + other_second.astype(jnp.float32)).astype(jnp.bfloat16),
        ],
        axis=1,
    )


SIZES = (8, 4, 2)


def along(axis):
    _, ys, cs = SIZES
    strides = (ys * cs, cs, 1)
    groups = {}
    for i in range(SIZES[0] * ys * cs):
        groups.setdefault(i - i // strides[axis] % SIZES[axis] * strides[axis], []).append(i)
    return list(groups.values())


def gather_near(passed):
    rows, mid = passed.shape[0], passed.shape[1] // 2
    piece = jnp.concatenate(
        [lax.ppermute(passed[:, :mid], "kvh", EVEN), lax.ppermute(passed[:, mid:], "kvh", ODD)],
        axis=1,
    )
    copies = jnp.broadcast_to(piece[None], (SIZES[0],) + piece.shape)
    line = lax.all_to_all(copies, "ctx", 0, 0, axis_index_groups=along(0)).reshape(-1, 2 * mid)
    plane = jnp.zeros((SIZES[1],) + line.shape, line.dtype)
    y = lax.axis_index("ctx") // SIZES[2] % SIZES[1]
    for step in range(SIZES[1]):
        pairs = [(group[(i + step) % SIZES[1]], group[i]) for group in along(1) for i in range(SIZES[1])]
        arrived = lax.ppermute(line, "ctx", pairs) if step else line
        plane = lax.dynamic_update_slice(plane, arrived[None], ((y + step) % SIZES[1], 0, 0))
    piece = plane.reshape(-1, 2 * mid)
    core = lax.axis_index("ctx") % 2
    other = lax.ppermute(piece, "ctx", [(i, i ^ 1) for i in range(lax.axis_size("ctx"))])
    whole = jnp.where(core == 0, jnp.stack([piece, other]), jnp.stack([other, piece]))
    return whole.reshape(-1, piece.shape[1])


def local(tokens, norm_gain, w_query, w_key, w_value, w_out, picks):
    me, block_index = lax.axis_index("kvh"), lax.axis_index("ctx")
    ctx_count = lax.axis_size("ctx")
    block_len = tokens.shape[0]
    half = block_len // 2
    chosen = picks[0, 0]

    wanted = lax.all_to_all(
        jnp.broadcast_to(chosen[None, None, 1:], (ctx_count, 1, 2)), "ctx", 0, 0
    ).reshape(ctx_count * 2)

    width = tokens.shape[1]
    from_left = lax.ppermute(tokens, "kvh", RIGHT)
    from_right = lax.ppermute(tokens, "kvh", LEFT)
    upper = lax.ppermute(from_left[:half], "kvh", RIGHT)
    lower = lax.ppermute(from_right[half:], "kvh", LEFT)

    def weights(w, place):
        start = place % RING * width
        rows = lax.dynamic_slice_in_dim(w, start, width, 0)
        return (rows * lax.dynamic_slice_in_dim(norm_gain, start, width, 0)[:, None]).astype(jnp.bfloat16)

    def project(columns):
        own, left, right, across = (weights(columns, me + step) for step in (0, 3, 1, 2))

        def times(rows, w):
            return jnp.dot(rows, w, preferred_element_type=jnp.float32)

        sofar = times(tokens, own) + times(from_left, left) + times(from_right, right)
        return sofar, sofar + jnp.concatenate([times(upper, across), times(lower, across)], axis=0)

    def squares(rows):
        return jnp.sum(jnp.square(rows.astype(jnp.float32)), axis=1, keepdims=True)

    square_sum = squares(tokens) + squares(from_left) + squares(from_right)
    square_sum += jnp.concatenate([squares(upper), squares(lower)], axis=0)
    scale = lax.rsqrt(square_sum / (RING * width) + 1e-05)

    positions = block_index * block_len + jnp.arange(block_len, dtype=jnp.int32)
    sofar, kv = project(jnp.concatenate([w_key, w_value], axis=1))
    kv = kv * scale
    key_rows = rotate_pairs(kv[:, None, :HD], positions)[:, 0].astype(jnp.bfloat16)
    own = jnp.concatenate([key_rows, kv[:, HD:].astype(jnp.bfloat16)], axis=0)
    held = lax.all_to_all(own.reshape(ctx_count, -1, HD), "ctx", 0, 0)
    before = lax.ppermute(own, "ctx", [(i, i + 1) for i in range(ctx_count - 1)])
    got = lax.all_to_all(route(wanted, held).reshape(ctx_count, 2, -1, HD), "ctx", 0, 0)

    zs, ys, cs = SIZES
    share = w_out.shape[0] // ctx_count
    place = (block_index % cs * ys + block_index // cs % ys) * zs + block_index // (ys * cs)
    w_near = gather_near(lax.dynamic_slice_in_dim(w_out, place * share, share, 0))

    queries = (project(w_query)[1] * scale).reshape(block_len, -1, HD)
    queries = rotate_pairs(queries, positions).astype(jnp.bfloat16).reshape(block_len, -1)
    flags = (chosen < block_index).astype(jnp.int32)
    sums, stats = attend_near(flags, queries, own, before)
    attended = attend_far(flags, queries, got, sums, stats)
    return project_out(attended, w_out, w_near, me)


def solution(mesh):
    in_specs = (
        P("ctx", "kvh"),
        P(),
        P(None, "kvh"),
        P(None, "kvh"),
        P(None, "kvh"),
        P("kvh", None),
        P("ctx", "kvh", None),
    )
    out_specs = P(("ctx", "kvh"), None)
    return jax.shard_map(local, mesh=mesh, in_specs=in_specs, out_specs=out_specs, check_vma=False)
```

```python
import jax
import jax.numpy as jnp
from jax import lax
from jax.experimental import pallas as pl
from jax.experimental.pallas import tpu as pltpu
from jax.sharding import PartitionSpec as P

HD = 128


ROPE_BASE = 500000.0


def rotate_pairs(head_rows, positions):
    half_dim = head_rows.shape[-1] // 2
    frequency = ROPE_BASE ** (-jnp.arange(half_dim, dtype=jnp.float32) * 2.0 / head_rows.shape[-1])
    angles = positions.astype(jnp.float32)[:, None] * frequency[None, :]
    cosine = jnp.cos(angles)[:, None, :]
    sine_part = jnp.sin(angles)[:, None, :]
    lower_half = head_rows[..., :half_dim]
    upper_half = head_rows[..., half_dim:]
    return jnp.concatenate(
        [
            lower_half * cosine - upper_half * sine_part,
            upper_half * cosine + lower_half * sine_part,
        ],
        axis=-1,
    )


SCALE = 1.4426950408889634 * HD**-0.5
MASKED = -1e30


def stack_heads(rows):
    return jnp.concatenate(
        [rows[:, h * HD : (h + 1) * HD] for h in range(rows.shape[1] // HD)], axis=0
    )


def scores_of(queries, keys):
    return lax.dot_general(
        queries, keys, (((1,), (1,)), ((), ())), preferred_element_type=jnp.float32
    )


def weigh(scores, offset, values):
    weights = jnp.exp2(scores * SCALE - offset).astype(jnp.bfloat16)
    wide = jnp.concatenate([values, jnp.ones_like(values)], axis=1)
    return jnp.dot(weights, wide, preferred_element_type=jnp.float32)


def row_max(scores):
    return jnp.max(scores, axis=1, keepdims=True)


def near_kernel(flag_ref, query_ref, own_ref, before_ref, sums_ref, stats_ref):
    block_len = query_ref.shape[0]
    quarter = block_len // RING
    heads = query_ref.shape[1] // HD
    stacked = quarter * heads
    has_before = flag_ref[0] > 0
    hidden = jnp.where(has_before, 0.0, -MASKED)
    row = lax.broadcasted_iota(jnp.int32, (stacked, quarter), 0) % quarter
    causal = lax.broadcasted_iota(jnp.int32, (stacked, quarter), 1) <= row
    left = lax.broadcasted_iota(jnp.int32, (stacked, HD), 1) < HD // 2
    for c in range(RING):
        start, end = c * quarter, (c + 1) * quarter
        queries = stack_heads(query_ref[start:end, :])
        own_scores = jnp.where(causal, scores_of(queries, own_ref[start:end, :]), MASKED)
        before_scores = scores_of(queries, before_ref[:block_len, :])
        top = jnp.maximum(
            row_max(own_scores), jnp.where(has_before, row_max(before_scores), MASKED)
        )
        if c:
            early_scores = scores_of(queries, own_ref[:start, :])
            top = jnp.maximum(top, row_max(early_scores))
        offset = top * SCALE
        sums = weigh(own_scores, offset, own_ref[block_len + start : block_len + end, :])
        sums += weigh(before_scores, offset + hidden, before_ref[block_len:, :])
        if c:
            sums += weigh(early_scores, offset, own_ref[block_len : block_len + start, :])
        rows = slice(c * stacked, (c + 1) * stacked)
        sums_ref[rows, :] = sums[:, :HD]
        stats_ref[rows, :] = jnp.where(left, sums[:, HD:], top)


def far_kernel(flag_ref, query_ref, got_ref, sums_ref, stats_ref, out_ref):
    block_len, width = query_ref.shape
    quarter = block_len // RING
    heads = width // HD
    stacked = quarter * heads
    pieces = got_ref.shape[0] // 2
    for c in range(RING):
        rows = slice(c * stacked, (c + 1) * stacked)
        queries = stack_heads(query_ref[c * quarter : (c + 1) * quarter, :])
        before_top = stats_ref[rows, HD // 2 : HD // 2 + 1]
        top, parts = before_top, []
        for r in range(2):
            scores = scores_of(queries, got_ref[:pieces, r].reshape(-1, HD))
            top = jnp.maximum(top, jnp.where(flag_ref[r + 1] > 0, row_max(scores), MASKED))
            parts.append(scores)
        offset = top * SCALE
        shrink = jnp.exp2((before_top - top) * SCALE)
        total = stats_ref[rows, :1] * shrink
        sums = sums_ref[rows, :] * shrink
        for r in range(2):
            hidden = jnp.where(flag_ref[r + 1] > 0, 0.0, -MASKED)
            more = weigh(parts[r], offset + hidden, got_ref[pieces:, r].reshape(-1, HD))
            sums += more[:, :HD]
            total += more[:, HD:]
        done = (sums / total).astype(jnp.bfloat16)
        for h in range(heads):
            out_ref[c * quarter : (c + 1) * quarter, h * HD : (h + 1) * HD] = done[
                h * quarter : (h + 1) * quarter
            ]


def query_kernel(
    me_ref, own_ref, left_ref, right_ref, upper_ref, lower_ref, w_ref, scale_ref, cos_ref, sin_ref, out_ref
):
    me = me_ref[0]
    half, depth = upper_ref.shape

    def rows(step):
        return w_ref[pl.ds(pl.multiple_of((me + step) % RING * depth, depth), depth), :]

    def times(chunk, w):
        return jnp.dot(chunk, w, preferred_element_type=jnp.float32)

    chunks = ((own_ref, rows(0)), (left_ref, rows(3)), (right_ref, rows(1)))
    across = rows(2)
    for part, last_ref in enumerate((upper_ref, lower_ref)):
        here = slice(part * half, (part + 1) * half)
        total = times(last_ref[...], across)
        for chunk_ref, w in chunks:
            total += times(chunk_ref[here, :], w)
        total *= scale_ref[here, :]
        for h in range(out_ref.shape[1] // HD):
            head = total[:, h * HD : (h + 1) * HD]
            turned = jnp.concatenate([head[:, HD // 2 :], head[:, : HD // 2]], axis=1)
            head = head * cos_ref[here, :] + turned * sin_ref[here, :]
            out_ref[here, h * HD : (h + 1) * HD] = head.astype(out_ref.dtype)


def route_kernel(wanted_ref, held_ref, out_ref):
    for i in range(out_ref.shape[0]):
        out_ref[i] = held_ref[wanted_ref[i]]


VMEM = pl.BlockSpec(memory_space=pltpu.VMEM)
SMEM = pl.BlockSpec(memory_space=pltpu.SMEM)


def call(kernel, out_shape, operands, flops, name, bytes_accessed=2**22):
    return pl.pallas_call(
        kernel,
        out_shape=out_shape,
        in_specs=[SMEM] + [VMEM] * (len(operands) - 1),
        out_specs=[VMEM] * len(out_shape),
        compiler_params=pltpu.CompilerParams(vmem_limit_bytes=40 * 2**20),
        cost_estimate=pl.CostEstimate(flops=flops, bytes_accessed=bytes_accessed, transcendentals=0),
        name=name,
    )(*operands)


def attend_near(flags, queries, own, before):
    block_len, width = queries.shape
    stacked = block_len * width // HD
    shape = jax.ShapeDtypeStruct((stacked, HD), jnp.float32)
    flops = 2**30
    return call(near_kernel, [shape, shape], (flags, queries, own, before), flops, "attend_near", 2**22)


def attend_far(flags, queries, got, sums, stats):
    block_len, width = queries.shape
    shape = jax.ShapeDtypeStruct((block_len, width), jnp.bfloat16)
    flops = 8 * block_len * width * block_len
    return call(far_kernel, [shape], (flags, queries, got, sums, stats), flops, "attend_far")[0]


def route(wanted, held):
    shape = jax.ShapeDtypeStruct(wanted.shape + held.shape[1:], held.dtype)
    return call(route_kernel, [shape], (wanted, held), 2**20, "route")[0]


RING = 4
RIGHT = [(i, (i + 1) % RING) for i in range(RING)]
LEFT = [(i, (i - 1) % RING) for i in range(RING)]
EVEN = [(i, i ^ 1) for i in range(RING)]
ODD = [(i, RING - 1 - i) for i in range(RING)]


def project_out(attended, w_out, w_near, me, core):
    rows, depth = attended.shape
    quarter, half = rows // RING, w_out.shape[1] // 2
    even, odd = me ^ 1, RING - 1 - me
    parts = attended.reshape(RING, quarter, depth)

    def pick(one, two):
        return jnp.concatenate(
            [
                lax.dynamic_index_in_dim(parts, one, 0, keepdims=False),
                lax.dynamic_index_in_dim(parts, two, 0, keepdims=False),
            ],
            axis=0,
        )

    across = (me + 2) % RING
    got_even = lax.ppermute(pick(even, across), "kvh", EVEN)
    got_odd = lax.ppermute(pick(odd, across), "kvh", ODD)

    def times(rows, w):
        return jnp.dot(rows, w, preferred_element_type=jnp.float32)

    def near(rows, columns):
        width = depth // 2
        mine = lax.dynamic_slice_in_dim(rows, core * width, width, 1)
        theirs = lax.dynamic_slice_in_dim(rows, (1 - core) * width, width, 1)
        return times(mine, w_near[0][:, columns]) + times(theirs, w_near[1][:, columns])

    front, back = slice(0, half), slice(half, None)

    def part(index):
        return lax.dynamic_index_in_dim(parts, index, 0, keepdims=False)

    sent_first = times(part(odd), w_out[:, :half]) + near(got_even[quarter:], front)
    sent_second = times(part(even), w_out[:, half:]) + near(got_odd[quarter:], back)
    other_first = lax.ppermute(sent_first.astype(jnp.bfloat16), "kvh", ODD)
    other_second = lax.ppermute(sent_second.astype(jnp.bfloat16), "kvh", EVEN)
    kept = times(part(me), w_out)
    kept_first = kept[:, :half] + near(got_even[:quarter], front)
    kept_second = kept[:, half:] + near(got_odd[:quarter], back)
    return jnp.concatenate(
        [
            (kept_first + other_first.astype(jnp.float32)).astype(jnp.bfloat16),
            (kept_second + other_second.astype(jnp.float32)).astype(jnp.bfloat16),
        ],
        axis=1,
    )


SIZES = (8, 4, 2)


def along(axis):
    _, ys, cs = SIZES
    strides = (ys * cs, cs, 1)
    groups = {}
    for i in range(SIZES[0] * ys * cs):
        groups.setdefault(i - i // strides[axis] % SIZES[axis] * strides[axis], []).append(i)
    return list(groups.values())


def after(value, *others):
    return lax.optimization_barrier((value, *others))[0]


def share_line(passed, ready, own):
    mid = passed.shape[1] // 2
    piece = jnp.concatenate(
        [lax.ppermute(passed[:, :mid], "kvh", EVEN), lax.ppermute(passed[:, mid:], "kvh", ODD)],
        axis=1,
    )
    share, size = piece.shape[0], SIZES[0]

    def fetch(rows, step):
        pairs = [(group[(i + step) % size], group[i]) for group in along(0) for i in range(size)]
        return lax.ppermute(rows, "ctx", pairs)

    trio = jnp.concatenate([fetch(piece, -1), piece, fetch(piece, 1)], axis=0)
    trio = after(trio, ready)
    found = jnp.concatenate([trio, fetch(trio, 3), fetch(trio[share:], -3)], axis=0)
    found = after(found, own)
    z = lax.axis_index("ctx") // (SIZES[1] * SIZES[2])
    place = (z + jnp.array([-1, 0, 1, 2, 3, 4, -3, -2])) % size
    place = (place[:, None] * share + jnp.arange(share)).reshape(-1)
    turn = (jnp.arange(size * share)[:, None] == place[None, :]).astype(found.dtype)
    return jnp.dot(turn, found, preferred_element_type=jnp.float32).astype(found.dtype)


def share_rest(line, ready, *last):
    plane = jnp.zeros((SIZES[1],) + line.shape, line.dtype)
    y = lax.axis_index("ctx") // SIZES[2] % SIZES[1]
    for step in range(SIZES[1]):
        pairs = [(group[(i + step) % SIZES[1]], group[i]) for group in along(1) for i in range(SIZES[1])]
        arrived = lax.ppermute(line, "ctx", pairs) if step else line
        arrived = after(arrived, ready)
        plane = lax.dynamic_update_slice(plane, arrived[None], ((y + step) % SIZES[1], 0, 0))
    plane = after(plane.reshape(-1, line.shape[1]), *last)
    return plane, lax.ppermute(plane, "ctx", [(i, i ^ 1) for i in range(lax.axis_size("ctx"))])


def local(tokens, norm_gain, w_query, w_key, w_value, w_out, picks):
    me, block_index = lax.axis_index("kvh"), lax.axis_index("ctx")
    ctx_count = lax.axis_size("ctx")
    block_len = tokens.shape[0]
    half = block_len // 2
    chosen = picks[0, 0]

    width = tokens.shape[1]
    from_left = lax.ppermute(tokens, "kvh", RIGHT)
    from_right = lax.ppermute(tokens, "kvh", LEFT)
    upper = lax.ppermute(from_left[:half], "kvh", RIGHT)
    lower = lax.ppermute(from_right[half:], "kvh", LEFT)

    def weights(w, place):
        start = place % RING * width
        rows = lax.dynamic_slice_in_dim(w, start, width, 0)
        return (rows * lax.dynamic_slice_in_dim(norm_gain, start, width, 0)[:, None]).astype(jnp.bfloat16)

    def project(columns, upper, lower):
        own, left, right, across = (weights(columns, me + step) for step in (0, 3, 1, 2))

        def times(rows, w):
            return jnp.dot(rows, w, preferred_element_type=jnp.float32)

        sofar = times(tokens, own) + times(from_left, left) + times(from_right, right)
        return sofar, sofar + jnp.concatenate([times(upper, across), times(lower, across)], axis=0)

    def squares(rows):
        return jnp.sum(jnp.square(rows.astype(jnp.float32)), axis=1, keepdims=True)

    square_sum = squares(tokens) + squares(from_left) + squares(from_right)
    square_sum += jnp.concatenate([squares(upper), squares(lower)], axis=0)
    scale = lax.rsqrt(square_sum / (RING * width) + 1e-05)

    positions = block_index * block_len + jnp.arange(block_len, dtype=jnp.int32)
    sofar, kv = project(jnp.concatenate([w_key, w_value], axis=1), upper, lower)
    kv = kv * scale

    wanted = lax.all_to_all(
        jnp.broadcast_to(chosen[None, None, 1:], (ctx_count, 1, 2)), "ctx", 0, 0
    ).reshape(ctx_count * 2)

    key_rows = rotate_pairs(kv[:, None, :HD], positions)[:, 0].astype(jnp.bfloat16)
    own = jnp.concatenate([key_rows, kv[:, HD:].astype(jnp.bfloat16)], axis=0)
    held = lax.all_to_all(own.reshape(ctx_count, -1, HD), "ctx", 0, 0)
    before = lax.ppermute(own, "ctx", [(i, i + 1) for i in range(ctx_count - 1)])
    sent = route(wanted, held)
    got = lax.all_to_all(sent.reshape(ctx_count, 2, -1, HD), "ctx", 0, 0)

    angles = positions.astype(jnp.float32)[:, None] * (
        ROPE_BASE ** (-jnp.arange(HD // 2, dtype=jnp.float32) * 2.0 / HD)
    )
    cosine, sine = jnp.cos(angles), jnp.sin(angles)
    queries = call(
        query_kernel,
        [jax.ShapeDtypeStruct((block_len, w_query.shape[1]), jnp.bfloat16)],
        (
            me[None],
            tokens,
            from_left,
            from_right,
            upper,
            lower,
            (w_query * norm_gain[:, None]).astype(jnp.bfloat16),
            jnp.broadcast_to(scale, (block_len, w_query.shape[1])),
            jnp.concatenate([cosine, cosine], axis=1),
            jnp.concatenate([-sine, sine], axis=1),
        ),
        2**31,
        "project_queries",
        2**23,
    )[0]
    flags = (chosen < block_index).astype(jnp.int32)
    sums, stats = attend_near(flags, queries, own, before)
    attended = attend_far(flags, queries, got, sums, stats)
    zs, ys, cs = SIZES
    share = w_out.shape[0] // ctx_count
    place = (block_index % cs * ys + block_index // cs % ys) * zs + block_index // (ys * cs)
    line = share_line(lax.dynamic_slice_in_dim(w_out, place * share, share, 0), sofar, upper)
    w_near = share_rest(line, own, attended)
    return project_out(attended, w_out, w_near, me, block_index % cs)


def solution(mesh):
    in_specs = (
        P("ctx", "kvh"),
        P(),
        P(None, "kvh"),
        P(None, "kvh"),
        P(None, "kvh"),
        P("kvh", None),
        P("ctx", "kvh", None),
    )
    out_specs = P(("ctx", "kvh"), None)
    return jax.shard_map(local, mesh=mesh, in_specs=in_specs, out_specs=out_specs, check_vma=False)
```

```python
import jax
import jax.numpy as jnp
from jax import lax
from jax.experimental import pallas as pl
from jax.experimental.pallas import tpu as pltpu
from jax.sharding import PartitionSpec as P

HD = 128


ROPE_BASE = 500000.0


def turns(positions):
    half_dim = HD // 2
    frequency = ROPE_BASE ** (-jnp.arange(half_dim, dtype=jnp.float32) * 2.0 / HD)
    angles = positions.astype(jnp.float32)[:, None] * frequency[None, :]
    return jnp.cos(angles), jnp.sin(angles)


def rotate_pairs(head_rows, cosine, sine):
    cosine, sine = cosine[:, None, :], sine[:, None, :]
    lower_half = head_rows[..., : HD // 2]
    upper_half = head_rows[..., HD // 2 :]
    return jnp.concatenate(
        [lower_half * cosine - upper_half * sine, upper_half * cosine + lower_half * sine],
        axis=-1,
    )


SCALE = 1.4426950408889634 * HD**-0.5
MASKED = -1e30


def stack_heads(rows):
    return jnp.concatenate(
        [rows[:, h * HD : (h + 1) * HD] for h in range(rows.shape[1] // HD)], axis=0
    )


def scores_of(queries, keys):
    return lax.dot_general(
        queries, keys, (((1,), (1,)), ((), ())), preferred_element_type=jnp.float32
    )


def weigh(scores, offset, values):
    weights = jnp.exp2(scores * SCALE - offset).astype(jnp.bfloat16)
    wide = jnp.concatenate([values, jnp.ones_like(values)], axis=1)
    return jnp.dot(weights, wide, preferred_element_type=jnp.float32)


def row_max(scores):
    return jnp.max(scores, axis=1, keepdims=True)


def near_kernel(flag_ref, query_ref, own_ref, before_ref, sums_ref, stats_ref):
    block_len = query_ref.shape[0]
    quarter = block_len // RING
    heads = query_ref.shape[1] // HD
    stacked = quarter * heads
    has_before = flag_ref[0] > 0
    hidden = jnp.where(has_before, 0.0, -MASKED)
    row = lax.broadcasted_iota(jnp.int32, (stacked, quarter), 0) % quarter
    causal = lax.broadcasted_iota(jnp.int32, (stacked, quarter), 1) <= row
    left = lax.broadcasted_iota(jnp.int32, (stacked, HD), 1) < HD // 2
    for c in range(RING):
        start, end = c * quarter, (c + 1) * quarter
        queries = stack_heads(query_ref[start:end, :])
        own_scores = jnp.where(causal, scores_of(queries, own_ref[start:end, :]), MASKED)
        before_scores = scores_of(queries, before_ref[:block_len, :])
        top = jnp.maximum(
            row_max(own_scores), jnp.where(has_before, row_max(before_scores), MASKED)
        )
        if c:
            early_scores = scores_of(queries, own_ref[:start, :])
            top = jnp.maximum(top, row_max(early_scores))
        offset = top * SCALE
        sums = weigh(own_scores, offset, own_ref[block_len + start : block_len + end, :])
        sums += weigh(before_scores, offset + hidden, before_ref[block_len:, :])
        if c:
            sums += weigh(early_scores, offset, own_ref[block_len : block_len + start, :])
        rows = slice(c * stacked, (c + 1) * stacked)
        sums_ref[rows, :] = sums[:, :HD]
        stats_ref[rows, :] = jnp.where(left, sums[:, HD:], top)


def far_kernel(flag_ref, query_ref, got_ref, sums_ref, stats_ref, out_ref):
    block_len, width = query_ref.shape
    quarter = block_len // RING
    heads = width // HD
    stacked = quarter * heads
    pieces = got_ref.shape[0] // 2
    for c in range(RING):
        rows = slice(c * stacked, (c + 1) * stacked)
        queries = stack_heads(query_ref[c * quarter : (c + 1) * quarter, :])
        before_top = stats_ref[rows, HD // 2 : HD // 2 + 1]
        top, parts = before_top, []
        for r in range(2):
            scores = scores_of(queries, got_ref[:pieces, r].reshape(-1, HD))
            top = jnp.maximum(top, jnp.where(flag_ref[r + 1] > 0, row_max(scores), MASKED))
            parts.append(scores)
        offset = top * SCALE
        shrink = jnp.exp2((before_top - top) * SCALE)
        total = stats_ref[rows, :1] * shrink
        sums = sums_ref[rows, :] * shrink
        for r in range(2):
            hidden = jnp.where(flag_ref[r + 1] > 0, 0.0, -MASKED)
            more = weigh(parts[r], offset + hidden, got_ref[pieces:, r].reshape(-1, HD))
            sums += more[:, :HD]
            total += more[:, HD:]
        done = (sums / total).astype(jnp.bfloat16)
        for h in range(heads):
            out_ref[c * quarter : (c + 1) * quarter, h * HD : (h + 1) * HD] = done[
                h * quarter : (h + 1) * quarter
            ]


def route_kernel(wanted_ref, held_ref, out_ref):
    for i in range(out_ref.shape[0]):
        out_ref[i] = held_ref[wanted_ref[i]]


VMEM = pl.BlockSpec(memory_space=pltpu.VMEM)
SMEM = pl.BlockSpec(memory_space=pltpu.SMEM)


def call(kernel, out_shape, operands, flops, name):
    return pl.pallas_call(
        kernel,
        out_shape=out_shape,
        in_specs=[SMEM] + [VMEM] * (len(operands) - 1),
        out_specs=[VMEM] * len(out_shape),
        compiler_params=pltpu.CompilerParams(vmem_limit_bytes=40 * 2**20),
        cost_estimate=pl.CostEstimate(flops=flops, bytes_accessed=2**22, transcendentals=2**21),
        name=name,
    )(*operands)


def attend_near(flags, queries, own, before):
    block_len, width = queries.shape
    stacked = block_len * width // HD
    shape = jax.ShapeDtypeStruct((stacked, HD), jnp.float32)
    flops = 8 * stacked * block_len * HD
    return call(near_kernel, [shape, shape], (flags, queries, own, before), flops, "attend_near")


def attend_far(flags, queries, got, sums, stats):
    block_len, width = queries.shape
    shape = jax.ShapeDtypeStruct((block_len, width), jnp.bfloat16)
    flops = 8 * block_len * width * block_len
    return call(far_kernel, [shape], (flags, queries, got, sums, stats), flops, "attend_far")[0]


def route(wanted, held):
    shape = jax.ShapeDtypeStruct(wanted.shape + held.shape[1:], held.dtype)
    return call(route_kernel, [shape], (wanted, held), 2**20, "route")[0]


RING = 4
RIGHT = [(i, (i + 1) % RING) for i in range(RING)]
LEFT = [(i, (i - 1) % RING) for i in range(RING)]
EVEN = [(i, i ^ 1) for i in range(RING)]
ODD = [(i, RING - 1 - i) for i in range(RING)]


def project_out(attended, w_out, w_near, me):
    rows, depth = attended.shape
    quarter, half = rows // RING, w_out.shape[1] // 2
    even, odd = me ^ 1, RING - 1 - me
    parts = attended.reshape(RING, quarter, depth)

    def pick(one, two):
        return jnp.concatenate(
            [
                lax.dynamic_index_in_dim(parts, one, 0, keepdims=False),
                lax.dynamic_index_in_dim(parts, two, 0, keepdims=False),
            ],
            axis=0,
        )

    across = (me + 2) % RING
    got_even = lax.ppermute(pick(even, across), "kvh", EVEN)
    got_odd = lax.ppermute(pick(odd, across), "kvh", ODD)

    def times(rows, w):
        return jnp.dot(rows, w, preferred_element_type=jnp.float32)

    def part(index):
        return lax.dynamic_index_in_dim(parts, index, 0, keepdims=False)

    sent_first = times(part(odd), w_out[:, :half]) + times(got_even[quarter:], w_near[:, :half])
    sent_second = times(part(even), w_out[:, half:]) + times(got_odd[quarter:], w_near[:, half:])
    other_first = lax.ppermute(sent_first.astype(jnp.bfloat16), "kvh", ODD)
    other_second = lax.ppermute(sent_second.astype(jnp.bfloat16), "kvh", EVEN)
    kept = times(part(me), w_out)
    kept_first = kept[:, :half] + times(got_even[:quarter], w_near[:, :half])
    kept_second = kept[:, half:] + times(got_odd[:quarter], w_near[:, half:])
    return jnp.concatenate(
        [
            (kept_first + other_first.astype(jnp.float32)).astype(jnp.bfloat16),
            (kept_second + other_second.astype(jnp.float32)).astype(jnp.bfloat16),
        ],
        axis=1,
    )


def after(value, *others):
    return lax.optimization_barrier((value, *others))[0]


def local(tokens, norm_gain, w_query, w_key, w_value, w_out, picks):
    me, block_index = lax.axis_index("kvh"), lax.axis_index("ctx")
    ctx_count = lax.axis_size("ctx")
    block_len = tokens.shape[0]
    half = block_len // 2
    chosen = picks[0, 0]

    wanted = lax.all_to_all(
        jnp.broadcast_to(chosen[None, None, 1:], (ctx_count, 1, 2)), "ctx", 0, 0
    ).reshape(ctx_count * 2)

    width = tokens.shape[1]
    from_left = lax.ppermute(tokens, "kvh", RIGHT)
    from_right = lax.ppermute(tokens, "kvh", LEFT)
    positions = block_index * block_len + jnp.arange(block_len, dtype=jnp.int32)
    cosine, sine = turns(positions)
    def weights(w, place):
        start = place % RING * width
        rows = lax.dynamic_slice_in_dim(w, start, width, 0)
        return (rows * lax.dynamic_slice_in_dim(norm_gain, start, width, 0)[:, None]).astype(jnp.bfloat16)

    def times(rows, w):
        return jnp.dot(rows, w, preferred_element_type=jnp.float32)

    w_kv = jnp.concatenate([w_key, w_value], axis=1)
    kv_own, query_own = times(tokens, weights(w_kv, me)), times(tokens, weights(w_query, me))
    kv_weights = [weights(w_kv, me + step) for step in (3, 1, 2)]
    from_left, from_right, wanted, cosine, kv_own, query_own, kv_weights = lax.optimization_barrier(
        (from_left, from_right, wanted, cosine, kv_own, query_own, kv_weights)
    )
    upper = lax.ppermute(from_left[:half], "kvh", RIGHT)
    lower = lax.ppermute(from_right[half:], "kvh", LEFT)

    def project(own, left, right, across):
        sofar = own + times(from_left, left) + times(from_right, right)
        return sofar + jnp.concatenate([times(upper, across), times(lower, across)], axis=0)

    def squares(rows):
        return jnp.sum(jnp.square(rows.astype(jnp.float32)), axis=1, keepdims=True)

    square_sum = squares(tokens) + squares(from_left) + squares(from_right)
    square_sum += jnp.concatenate([squares(upper), squares(lower)], axis=0)
    scale = lax.rsqrt(square_sum / (RING * width) + 1e-05)

    kv = project(kv_own, *kv_weights) * scale
    key_rows = rotate_pairs(kv[:, None, :HD], cosine, sine)[:, 0].astype(jnp.bfloat16)
    own = jnp.concatenate([key_rows, kv[:, HD:].astype(jnp.bfloat16)], axis=0)
    held = lax.all_to_all(own.reshape(ctx_count, -1, HD), "ctx", 0, 0)
    before = lax.ppermute(own, "ctx", [(i, i + 1) for i in range(ctx_count - 1)])
    got = lax.all_to_all(route(wanted, held).reshape(ctx_count, 2, -1, HD), "ctx", 0, 0)

    share = w_out.shape[0] // ctx_count
    passed = lax.dynamic_slice_in_dim(w_out, block_index * share, share, 0)
    mid = w_out.shape[1] // 2
    passed = jnp.concatenate(
        [lax.ppermute(passed[:, :mid], "kvh", EVEN), lax.ppermute(passed[:, mid:], "kvh", ODD)],
        axis=1,
    )
    w_near = lax.all_gather(after(passed, from_left, from_right), "ctx", axis=0, tiled=True)

    queries = (project(query_own, *(weights(w_query, me + step) for step in (3, 1, 2))) * scale).reshape(block_len, -1, HD)
    queries = rotate_pairs(queries, cosine, sine).astype(jnp.bfloat16).reshape(block_len, -1)
    flags = (chosen < block_index).astype(jnp.int32)
    sums, stats = attend_near(flags, queries, own, before)
    attended = attend_far(flags, queries, got, sums, stats)
    return project_out(attended, w_out, w_near, me)


def solution(mesh):
    in_specs = (
        P("ctx", "kvh"),
        P(),
        P(None, "kvh"),
        P(None, "kvh"),
        P(None, "kvh"),
        P("kvh", None),
        P("ctx", "kvh", None),
    )
    out_specs = P(("ctx", "kvh"), None)
    return jax.shard_map(local, mesh=mesh, in_specs=in_specs, out_specs=out_specs, check_vma=False)
```

```python
import jax
import jax.numpy as jnp
from jax import lax
from jax.experimental import pallas as pl
from jax.experimental.pallas import tpu as pltpu
from jax.sharding import PartitionSpec as P

HD = 128


ROPE_BASE = 500000.0


def turns(positions):
    half_dim = HD // 2
    frequency = ROPE_BASE ** (-jnp.arange(half_dim, dtype=jnp.float32) * 2.0 / HD)
    angles = positions.astype(jnp.float32)[:, None] * frequency[None, :]
    return jnp.cos(angles), jnp.sin(angles)


def rotate_pairs(head_rows, cosine, sine):
    cosine, sine = cosine[:, None, :], sine[:, None, :]
    lower_half = head_rows[..., : HD // 2]
    upper_half = head_rows[..., HD // 2 :]
    return jnp.concatenate(
        [lower_half * cosine - upper_half * sine, upper_half * cosine + lower_half * sine],
        axis=-1,
    )


SCALE = 1.4426950408889634 * HD**-0.5
MASKED = -1e30


def stack_heads(rows):
    return jnp.concatenate(
        [rows[:, h * HD : (h + 1) * HD] for h in range(rows.shape[1] // HD)], axis=0
    )


def scores_of(queries, keys):
    return lax.dot_general(
        queries, keys, (((1,), (1,)), ((), ())), preferred_element_type=jnp.float32
    )


def weigh(scores, offset, values):
    weights = jnp.exp2(scores * SCALE - offset).astype(jnp.bfloat16)
    wide = jnp.concatenate([values, jnp.ones_like(values)], axis=1)
    return jnp.dot(weights, wide, preferred_element_type=jnp.float32)


def row_max(scores):
    return jnp.max(scores, axis=1, keepdims=True)


def near_kernel(flag_ref, query_ref, own_ref, before_ref, sums_ref, stats_ref):
    block_len = query_ref.shape[0]
    quarter = block_len // RING
    heads = query_ref.shape[1] // HD
    stacked = quarter * heads
    has_before = flag_ref[0] > 0
    hidden = jnp.where(has_before, 0.0, -MASKED)
    row = lax.broadcasted_iota(jnp.int32, (stacked, quarter), 0) % quarter
    causal = lax.broadcasted_iota(jnp.int32, (stacked, quarter), 1) <= row
    left = lax.broadcasted_iota(jnp.int32, (stacked, HD), 1) < HD // 2
    for c in range(RING):
        start, end = c * quarter, (c + 1) * quarter
        queries = stack_heads(query_ref[start:end, :])
        own_scores = jnp.where(causal, scores_of(queries, own_ref[start:end, :]), MASKED)
        before_scores = scores_of(queries, before_ref[:block_len, :])
        top = jnp.maximum(
            row_max(own_scores), jnp.where(has_before, row_max(before_scores), MASKED)
        )
        if c:
            early_scores = scores_of(queries, own_ref[:start, :])
            top = jnp.maximum(top, row_max(early_scores))
        offset = top * SCALE
        sums = weigh(own_scores, offset, own_ref[block_len + start : block_len + end, :])
        sums += weigh(before_scores, offset + hidden, before_ref[block_len:, :])
        if c:
            sums += weigh(early_scores, offset, own_ref[block_len : block_len + start, :])
        rows = slice(c * stacked, (c + 1) * stacked)
        sums_ref[rows, :] = sums[:, :HD]
        stats_ref[rows, :] = jnp.where(left, sums[:, HD:], top)


def far_kernel(flag_ref, query_ref, got_ref, sums_ref, stats_ref, out_ref):
    block_len, width = query_ref.shape
    quarter = block_len // RING
    heads = width // HD
    stacked = quarter * heads
    pieces = got_ref.shape[0] // 2
    for c in range(RING):
        rows = slice(c * stacked, (c + 1) * stacked)
        queries = stack_heads(query_ref[c * quarter : (c + 1) * quarter, :])
        before_top = stats_ref[rows, HD // 2 : HD // 2 + 1]
        top, parts = before_top, []
        for r in range(2):
            scores = scores_of(queries, got_ref[:pieces, r].reshape(-1, HD))
            top = jnp.maximum(top, jnp.where(flag_ref[r + 1] > 0, row_max(scores), MASKED))
            parts.append(scores)
        offset = top * SCALE
        shrink = jnp.exp2((before_top - top) * SCALE)
        total = stats_ref[rows, :1] * shrink
        sums = sums_ref[rows, :] * shrink
        for r in range(2):
            hidden = jnp.where(flag_ref[r + 1] > 0, 0.0, -MASKED)
            more = weigh(parts[r], offset + hidden, got_ref[pieces:, r].reshape(-1, HD))
            sums += more[:, :HD]
            total += more[:, HD:]
        done = (sums / total).astype(jnp.bfloat16)
        for h in range(heads):
            out_ref[c * quarter : (c + 1) * quarter, h * HD : (h + 1) * HD] = done[
                h * quarter : (h + 1) * quarter
            ]


def route_kernel(wanted_ref, held_ref, out_ref):
    for i in range(out_ref.shape[0]):
        out_ref[i] = held_ref[wanted_ref[i]]


VMEM = pl.BlockSpec(memory_space=pltpu.VMEM)
SMEM = pl.BlockSpec(memory_space=pltpu.SMEM)


def call(kernel, out_shape, operands, flops, name):
    return pl.pallas_call(
        kernel,
        out_shape=out_shape,
        in_specs=[SMEM] + [VMEM] * (len(operands) - 1),
        out_specs=[VMEM] * len(out_shape),
        compiler_params=pltpu.CompilerParams(vmem_limit_bytes=40 * 2**20),
        cost_estimate=pl.CostEstimate(flops=flops, bytes_accessed=2**22, transcendentals=2**21),
        name=name,
    )(*operands)


def attend_near(flags, queries, own, before):
    block_len, width = queries.shape
    stacked = block_len * width // HD
    shape = jax.ShapeDtypeStruct((stacked, HD), jnp.float32)
    flops = 8 * stacked * block_len * HD
    return call(near_kernel, [shape, shape], (flags, queries, own, before), flops, "attend_near")


def attend_far(flags, queries, got, sums, stats):
    block_len, width = queries.shape
    shape = jax.ShapeDtypeStruct((block_len, width), jnp.bfloat16)
    flops = 8 * block_len * width * block_len
    return call(far_kernel, [shape], (flags, queries, got, sums, stats), flops, "attend_far")[0]


def route(wanted, held):
    shape = jax.ShapeDtypeStruct(wanted.shape + held.shape[1:], held.dtype)
    return call(route_kernel, [shape], (wanted, held), 2**20, "route")[0]


RING = 4
RIGHT = [(i, (i + 1) % RING) for i in range(RING)]
LEFT = [(i, (i - 1) % RING) for i in range(RING)]
EVEN = [(i, i ^ 1) for i in range(RING)]
ODD = [(i, RING - 1 - i) for i in range(RING)]


def project_out(attended, w_out, w_near, me):
    rows, depth = attended.shape
    quarter, half = rows // RING, w_out.shape[1] // 2
    even, odd = me ^ 1, RING - 1 - me
    parts = attended.reshape(RING, quarter, depth)

    def pick(one, two):
        return jnp.concatenate(
            [
                lax.dynamic_index_in_dim(parts, one, 0, keepdims=False),
                lax.dynamic_index_in_dim(parts, two, 0, keepdims=False),
            ],
            axis=0,
        )

    across = (me + 2) % RING
    got_even = lax.ppermute(pick(even, across), "kvh", EVEN)
    got_odd = lax.ppermute(pick(odd, across), "kvh", ODD)

    def times(rows, w):
        return jnp.dot(rows, w, preferred_element_type=jnp.float32)

    def part(index):
        return lax.dynamic_index_in_dim(parts, index, 0, keepdims=False)

    sent_first = times(part(odd), w_out[:, :half]) + times(got_even[quarter:], w_near[0])
    sent_second = times(part(even), w_out[:, half:]) + times(got_odd[quarter:], w_near[1])
    other_first = lax.ppermute(sent_first.astype(jnp.bfloat16), "kvh", ODD)
    other_second = lax.ppermute(sent_second.astype(jnp.bfloat16), "kvh", EVEN)
    kept = times(part(me), w_out)
    kept_first = kept[:, :half] + times(got_even[:quarter], w_near[0])
    kept_second = kept[:, half:] + times(got_odd[:quarter], w_near[1])
    return jnp.concatenate(
        [
            (kept_first + other_first.astype(jnp.float32)).astype(jnp.bfloat16),
            (kept_second + other_second.astype(jnp.float32)).astype(jnp.bfloat16),
        ],
        axis=1,
    )


def after(value, *others):
    return lax.optimization_barrier((value, *others))[0]


def local(tokens, norm_gain, w_query, w_key, w_value, w_out, picks):
    me, block_index = lax.axis_index("kvh"), lax.axis_index("ctx")
    ctx_count = lax.axis_size("ctx")
    block_len = tokens.shape[0]
    half = block_len // 2
    chosen = picks[0, 0]

    wanted = lax.all_to_all(
        jnp.broadcast_to(chosen[None, None, 1:], (ctx_count, 1, 2)), "ctx", 0, 0
    ).reshape(ctx_count * 2)

    width = tokens.shape[1]
    from_left = lax.ppermute(tokens, "kvh", RIGHT)
    from_right = lax.ppermute(tokens, "kvh", LEFT)
    positions = block_index * block_len + jnp.arange(block_len, dtype=jnp.int32)
    cosine, sine = turns(positions)
    def weights(w, place):
        start = place % RING * width
        rows = lax.dynamic_slice_in_dim(w, start, width, 0)
        return (rows * lax.dynamic_slice_in_dim(norm_gain, start, width, 0)[:, None]).astype(jnp.bfloat16)

    def times(rows, w):
        return jnp.dot(rows, w, preferred_element_type=jnp.float32)

    w_kv = jnp.concatenate([w_key, w_value], axis=1)
    kv_own, query_own = times(tokens, weights(w_kv, me)), times(tokens, weights(w_query, me))
    kv_weights = [weights(w_kv, me + step) for step in (3, 1, 2)]
    from_left, from_right, wanted, cosine, kv_own, query_own, kv_weights = lax.optimization_barrier(
        (from_left, from_right, wanted, cosine, kv_own, query_own, kv_weights)
    )
    upper = lax.ppermute(from_left[:half], "kvh", RIGHT)
    lower = lax.ppermute(from_right[half:], "kvh", LEFT)

    def project(own, left, right, across):
        sofar = own + times(from_left, left) + times(from_right, right)
        return sofar + jnp.concatenate([times(upper, across), times(lower, across)], axis=0)

    def squares(rows):
        return jnp.sum(jnp.square(rows.astype(jnp.float32)), axis=1, keepdims=True)

    square_sum = squares(tokens) + squares(from_left) + squares(from_right)
    square_sum += jnp.concatenate([squares(upper), squares(lower)], axis=0)
    scale = lax.rsqrt(square_sum / (RING * width) + 1e-05)

    kv = project(kv_own, *kv_weights) * scale
    key_rows = rotate_pairs(kv[:, None, :HD], cosine, sine)[:, 0].astype(jnp.bfloat16)
    own = jnp.concatenate([key_rows, kv[:, HD:].astype(jnp.bfloat16)], axis=0)
    held = lax.all_to_all(own.reshape(ctx_count, -1, HD), "ctx", 0, 0)
    before = lax.ppermute(own, "ctx", [(i, i + 1) for i in range(ctx_count - 1)])
    got = lax.all_to_all(route(wanted, held).reshape(ctx_count, 2, -1, HD), "ctx", 0, 0)

    mid = w_out.shape[1] // 2
    passed = after(w_out, own)
    w_near = lax.ppermute(passed[:, :mid], "kvh", EVEN), lax.ppermute(passed[:, mid:], "kvh", ODD)

    queries = (project(query_own, *(weights(w_query, me + step) for step in (3, 1, 2))) * scale).reshape(block_len, -1, HD)
    queries = rotate_pairs(queries, cosine, sine).astype(jnp.bfloat16).reshape(block_len, -1)
    flags = (chosen < block_index).astype(jnp.int32)
    sums, stats = attend_near(flags, queries, own, before)
    attended = attend_far(flags, queries, got, sums, stats)
    return project_out(attended, w_out, w_near, me)


def solution(mesh):
    in_specs = (
        P("ctx", "kvh"),
        P(),
        P(None, "kvh"),
        P(None, "kvh"),
        P(None, "kvh"),
        P("kvh", None),
        P("ctx", "kvh", None),
    )
    out_specs = P(("ctx", "kvh"), None)
    return jax.shard_map(local, mesh=mesh, in_specs=in_specs, out_specs=out_specs, check_vma=False)
```

```python
import jax
import jax.numpy as jnp
from jax import lax
from jax.experimental import pallas as pl
from jax.experimental.pallas import tpu as pltpu
from jax.sharding import PartitionSpec as P

HD = 128


ROPE_BASE = 500000.0


def turns(positions):
    half_dim = HD // 2
    frequency = ROPE_BASE ** (-jnp.arange(half_dim, dtype=jnp.float32) * 2.0 / HD)
    angles = positions.astype(jnp.float32)[:, None] * frequency[None, :]
    return jnp.cos(angles), jnp.sin(angles)


def rotate_pairs(head_rows, cosine, sine):
    cosine, sine = cosine[:, None, :], sine[:, None, :]
    lower_half = head_rows[..., : HD // 2]
    upper_half = head_rows[..., HD // 2 :]
    return jnp.concatenate(
        [lower_half * cosine - upper_half * sine, upper_half * cosine + lower_half * sine],
        axis=-1,
    )


SCALE = 1.4426950408889634 * HD**-0.5
MASKED = -1e30


def stack_heads(rows):
    return jnp.concatenate(
        [rows[:, h * HD : (h + 1) * HD] for h in range(rows.shape[1] // HD)], axis=0
    )


def scores_of(queries, keys):
    return lax.dot_general(
        queries, keys, (((1,), (1,)), ((), ())), preferred_element_type=jnp.float32
    )


def weigh(scores, offset, values):
    weights = jnp.exp2(scores * SCALE - offset).astype(jnp.bfloat16)
    wide = jnp.concatenate([values, jnp.ones_like(values)], axis=1)
    return jnp.dot(weights, wide, preferred_element_type=jnp.float32)


def row_max(scores):
    return jnp.max(scores, axis=1, keepdims=True)


def near_kernel(flag_ref, query_ref, own_ref, before_ref, sums_ref, stats_ref):
    block_len = query_ref.shape[0]
    quarter = block_len // RING
    heads = query_ref.shape[1] // HD
    stacked = quarter * heads
    has_before = flag_ref[0] > 0
    hidden = jnp.where(has_before, 0.0, -MASKED)
    row = lax.broadcasted_iota(jnp.int32, (stacked, quarter), 0) % quarter
    causal = lax.broadcasted_iota(jnp.int32, (stacked, quarter), 1) <= row
    left = lax.broadcasted_iota(jnp.int32, (stacked, HD), 1) < HD // 2
    for c in range(RING):
        start, end = c * quarter, (c + 1) * quarter
        queries = stack_heads(query_ref[start:end, :])
        own_scores = jnp.where(causal, scores_of(queries, own_ref[start:end, :]), MASKED)
        before_scores = scores_of(queries, before_ref[:block_len, :])
        top = jnp.maximum(
            row_max(own_scores), jnp.where(has_before, row_max(before_scores), MASKED)
        )
        if c:
            early_scores = scores_of(queries, own_ref[:start, :])
            top = jnp.maximum(top, row_max(early_scores))
        offset = top * SCALE
        sums = weigh(own_scores, offset, own_ref[block_len + start : block_len + end, :])
        sums += weigh(before_scores, offset + hidden, before_ref[block_len:, :])
        if c:
            sums += weigh(early_scores, offset, own_ref[block_len : block_len + start, :])
        rows = slice(c * stacked, (c + 1) * stacked)
        sums_ref[rows, :] = sums[:, :HD]
        stats_ref[rows, :] = jnp.where(left, sums[:, HD:], top)


def far_kernel(flag_ref, query_ref, got_ref, sums_ref, stats_ref, out_ref):
    block_len, width = query_ref.shape
    quarter = block_len // RING
    heads = width // HD
    stacked = quarter * heads
    pieces = got_ref.shape[0] // 2
    for c in range(RING):
        rows = slice(c * stacked, (c + 1) * stacked)
        queries = stack_heads(query_ref[c * quarter : (c + 1) * quarter, :])
        before_top = stats_ref[rows, HD // 2 : HD // 2 + 1]
        top, parts = before_top, []
        for r in range(2):
            scores = scores_of(queries, got_ref[:pieces, r].reshape(-1, HD))
            top = jnp.maximum(top, jnp.where(flag_ref[r + 1] > 0, row_max(scores), MASKED))
            parts.append(scores)
        offset = top * SCALE
        shrink = jnp.exp2((before_top - top) * SCALE)
        total = stats_ref[rows, :1] * shrink
        sums = sums_ref[rows, :] * shrink
        for r in range(2):
            hidden = jnp.where(flag_ref[r + 1] > 0, 0.0, -MASKED)
            more = weigh(parts[r], offset + hidden, got_ref[pieces:, r].reshape(-1, HD))
            sums += more[:, :HD]
            total += more[:, HD:]
        done = (sums / total).astype(jnp.bfloat16)
        for h in range(heads):
            out_ref[c * quarter : (c + 1) * quarter, h * HD : (h + 1) * HD] = done[
                h * quarter : (h + 1) * quarter
            ]


def route_kernel(wanted_ref, held_ref, out_ref):
    for i in range(out_ref.shape[0]):
        out_ref[i] = held_ref[wanted_ref[i]]


VMEM = pl.BlockSpec(memory_space=pltpu.VMEM)
SMEM = pl.BlockSpec(memory_space=pltpu.SMEM)


def call(kernel, out_shape, operands, flops, name):
    return pl.pallas_call(
        kernel,
        out_shape=out_shape,
        in_specs=[SMEM] + [VMEM] * (len(operands) - 1),
        out_specs=[VMEM] * len(out_shape),
        compiler_params=pltpu.CompilerParams(vmem_limit_bytes=40 * 2**20),
        cost_estimate=pl.CostEstimate(flops=flops, bytes_accessed=2**22, transcendentals=2**21),
        name=name,
    )(*operands)


def attend_near(flags, queries, own, before):
    block_len, width = queries.shape
    stacked = block_len * width // HD
    shape = jax.ShapeDtypeStruct((stacked, HD), jnp.float32)
    flops = 8 * stacked * block_len * HD
    return call(near_kernel, [shape, shape], (flags, queries, own, before), flops, "attend_near")


def attend_far(flags, queries, got, sums, stats):
    block_len, width = queries.shape
    shape = jax.ShapeDtypeStruct((block_len, width), jnp.bfloat16)
    flops = 8 * block_len * width * block_len
    return call(far_kernel, [shape], (flags, queries, got, sums, stats), flops, "attend_far")[0]


def route(wanted, held):
    shape = jax.ShapeDtypeStruct(wanted.shape + held.shape[1:], held.dtype)
    return call(route_kernel, [shape], (wanted, held), 2**20, "route")[0]


RING = 4
RIGHT = [(i, (i + 1) % RING) for i in range(RING)]
LEFT = [(i, (i - 1) % RING) for i in range(RING)]
EVEN = [(i, i ^ 1) for i in range(RING)]
ODD = [(i, RING - 1 - i) for i in range(RING)]


def project_out(attended, w_out, w_near, me):
    rows, depth = attended.shape
    quarter, half = rows // RING, w_out.shape[1] // 2
    even, odd = me ^ 1, RING - 1 - me
    parts = attended.reshape(RING, quarter, depth)

    def pick(one, two):
        return jnp.concatenate(
            [
                lax.dynamic_index_in_dim(parts, one, 0, keepdims=False),
                lax.dynamic_index_in_dim(parts, two, 0, keepdims=False),
            ],
            axis=0,
        )

    across = (me + 2) % RING
    got_even = lax.ppermute(pick(even, across), "kvh", EVEN)
    got_odd = lax.ppermute(pick(odd, across), "kvh", ODD)

    def times(rows, w):
        return jnp.dot(rows, w, preferred_element_type=jnp.float32)

    def part(index):
        return lax.dynamic_index_in_dim(parts, index, 0, keepdims=False)

    sent_first = times(part(odd), w_out[:, :half]) + times(got_even[quarter:], w_near[0])
    sent_second = times(part(even), w_out[:, half:]) + times(got_odd[quarter:], w_near[1])
    other_first = lax.ppermute(sent_first.astype(jnp.bfloat16), "kvh", ODD)
    other_second = lax.ppermute(sent_second.astype(jnp.bfloat16), "kvh", EVEN)
    kept = times(part(me), w_out)
    kept_first = kept[:, :half] + times(got_even[:quarter], w_near[0])
    kept_second = kept[:, half:] + times(got_odd[:quarter], w_near[1])
    return jnp.concatenate(
        [
            (kept_first + other_first.astype(jnp.float32)).astype(jnp.bfloat16),
            (kept_second + other_second.astype(jnp.float32)).astype(jnp.bfloat16),
        ],
        axis=1,
    )


def after(value, *others):
    return lax.optimization_barrier((value, *others))[0]


def local(tokens, norm_gain, w_query, w_key, w_value, w_out, picks):
    me, block_index = lax.axis_index("kvh"), lax.axis_index("ctx")
    ctx_count = lax.axis_size("ctx")
    block_len = tokens.shape[0]
    half = block_len // 2
    chosen = picks[0, 0]

    wanted = lax.all_to_all(
        jnp.broadcast_to(chosen[None, None, 1:], (ctx_count, 1, 2)), "ctx", 0, 0
    ).reshape(ctx_count * 2)

    width = tokens.shape[1]
    from_left = lax.ppermute(tokens, "kvh", RIGHT)
    from_right = lax.ppermute(tokens, "kvh", LEFT)
    positions = block_index * block_len + jnp.arange(block_len, dtype=jnp.int32)
    cosine, sine = turns(positions)
    def weights(w, place):
        start = place % RING * width
        rows = lax.dynamic_slice_in_dim(w, start, width, 0)
        return (rows * lax.dynamic_slice_in_dim(norm_gain, start, width, 0)[:, None]).astype(jnp.bfloat16)

    def times(rows, w):
        return jnp.dot(rows, w, preferred_element_type=jnp.float32)

    w_kv = jnp.concatenate([w_key, w_value], axis=1)
    kv_own = times(tokens, weights(w_kv, me))
    kv_weights = [weights(w_kv, me + step) for step in (3, 1, 2)]
    from_left, from_right, wanted, cosine, kv_own, kv_weights = lax.optimization_barrier(
        (from_left, from_right, wanted, cosine, kv_own, kv_weights)
    )
    upper = lax.ppermute(from_left[:half], "kvh", RIGHT)
    lower = lax.ppermute(from_right[half:], "kvh", LEFT)

    def project(own, left, right, across):
        sofar = own + times(from_left, left) + times(from_right, right)
        return sofar + jnp.concatenate([times(upper, across), times(lower, across)], axis=0)

    def squares(rows):
        return jnp.sum(jnp.square(rows.astype(jnp.float32)), axis=1, keepdims=True)

    square_sum = squares(tokens) + squares(from_left) + squares(from_right)
    square_sum += jnp.concatenate([squares(upper), squares(lower)], axis=0)
    scale = lax.rsqrt(square_sum / (RING * width) + 1e-05)

    kv = project(kv_own, *kv_weights) * scale
    key_rows = rotate_pairs(kv[:, None, :HD], cosine, sine)[:, 0].astype(jnp.bfloat16)
    own = jnp.concatenate([key_rows, kv[:, HD:].astype(jnp.bfloat16)], axis=0)
    held = lax.all_to_all(own.reshape(ctx_count, -1, HD), "ctx", 0, 0)
    before = lax.ppermute(own, "ctx", [(i, i + 1) for i in range(ctx_count - 1)])
    got = lax.all_to_all(route(wanted, held).reshape(ctx_count, 2, -1, HD), "ctx", 0, 0)

    mid = w_out.shape[1] // 2
    passed = after(w_out, from_left)
    front, back = after(passed[:, :mid], upper, lower), after(passed[:, mid:], upper, lower)
    w_near = lax.ppermute(front, "kvh", EVEN), lax.ppermute(back, "kvh", ODD)

    w_late = after(w_query, from_left)
    queries = (project(
        times(tokens, weights(w_late, me)), *(weights(w_late, me + step) for step in (3, 1, 2))
    ) * scale).reshape(block_len, -1, HD)
    queries = rotate_pairs(queries, cosine, sine).astype(jnp.bfloat16).reshape(block_len, -1)
    flags = (chosen < block_index).astype(jnp.int32)
    sums, stats = attend_near(flags, queries, own, before)
    attended = attend_far(flags, queries, got, sums, stats)
    return project_out(attended, w_out, w_near, me)


def solution(mesh):
    in_specs = (
        P("ctx", "kvh"),
        P(),
        P(None, "kvh"),
        P(None, "kvh"),
        P(None, "kvh"),
        P("kvh", None),
        P("ctx", "kvh", None),
    )
    out_specs = P(("ctx", "kvh"), None)
    return jax.shard_map(local, mesh=mesh, in_specs=in_specs, out_specs=out_specs, check_vma=False)
```

```python
import jax
import jax.numpy as jnp
from jax import lax
from jax.experimental import pallas as pl
from jax.experimental.pallas import tpu as pltpu
from jax.sharding import PartitionSpec as P

HD = 128


ROPE_BASE = 500000.0


def turns(positions):
    half_dim = HD // 2
    frequency = ROPE_BASE ** (-jnp.arange(half_dim, dtype=jnp.float32) * 2.0 / HD)
    angles = positions.astype(jnp.float32)[:, None] * frequency[None, :]
    return jnp.cos(angles), jnp.sin(angles)


def rotate_pairs(head_rows, cosine, sine):
    cosine, sine = cosine[:, None, :], sine[:, None, :]
    lower_half = head_rows[..., : HD // 2]
    upper_half = head_rows[..., HD // 2 :]
    return jnp.concatenate(
        [lower_half * cosine - upper_half * sine, upper_half * cosine + lower_half * sine],
        axis=-1,
    )


SCALE = 1.4426950408889634 * HD**-0.5
MASKED = -1e30


def stack_heads(rows):
    return jnp.concatenate(
        [rows[:, h * HD : (h + 1) * HD] for h in range(rows.shape[1] // HD)], axis=0
    )


def scores_of(queries, keys):
    return lax.dot_general(
        queries, keys, (((1,), (1,)), ((), ())), preferred_element_type=jnp.float32
    )


def weigh(scores, offset, values):
    weights = jnp.exp2(scores * SCALE - offset).astype(jnp.bfloat16)
    wide = jnp.concatenate([values, jnp.ones_like(values)], axis=1)
    return jnp.dot(weights, wide, preferred_element_type=jnp.float32)


def row_max(scores):
    return jnp.max(scores, axis=1, keepdims=True)


def near_kernel(flag_ref, query_ref, own_ref, before_ref, sums_ref, stats_ref):
    block_len = query_ref.shape[0]
    quarter = block_len // RING
    heads = query_ref.shape[1] // HD
    stacked = quarter * heads
    has_before = flag_ref[0] > 0
    hidden = jnp.where(has_before, 0.0, -MASKED)
    row = lax.broadcasted_iota(jnp.int32, (stacked, quarter), 0) % quarter
    causal = lax.broadcasted_iota(jnp.int32, (stacked, quarter), 1) <= row
    left = lax.broadcasted_iota(jnp.int32, (stacked, HD), 1) < HD // 2
    for c in range(RING):
        start, end = c * quarter, (c + 1) * quarter
        queries = stack_heads(query_ref[start:end, :])
        own_scores = jnp.where(causal, scores_of(queries, own_ref[start:end, :]), MASKED)
        before_scores = scores_of(queries, before_ref[:block_len, :])
        top = jnp.maximum(
            row_max(own_scores), jnp.where(has_before, row_max(before_scores), MASKED)
        )
        if c:
            early_scores = scores_of(queries, own_ref[:start, :])
            top = jnp.maximum(top, row_max(early_scores))
        offset = top * SCALE
        sums = weigh(own_scores, offset, own_ref[block_len + start : block_len + end, :])
        sums += weigh(before_scores, offset + hidden, before_ref[block_len:, :])
        if c:
            sums += weigh(early_scores, offset, own_ref[block_len : block_len + start, :])
        rows = slice(c * stacked, (c + 1) * stacked)
        sums_ref[rows, :] = sums[:, :HD]
        stats_ref[rows, :] = jnp.where(left, sums[:, HD:], top)


def far_kernel(flag_ref, query_ref, got_ref, sums_ref, stats_ref, out_ref):
    block_len, width = query_ref.shape
    quarter = block_len // RING
    heads = width // HD
    stacked = quarter * heads
    pieces = got_ref.shape[0] // 2
    for c in range(RING):
        rows = slice(c * stacked, (c + 1) * stacked)
        queries = stack_heads(query_ref[c * quarter : (c + 1) * quarter, :])
        before_top = stats_ref[rows, HD // 2 : HD // 2 + 1]
        top, parts = before_top, []
        for r in range(2):
            scores = scores_of(queries, got_ref[:pieces, r].reshape(-1, HD))
            top = jnp.maximum(top, jnp.where(flag_ref[r + 1] > 0, row_max(scores), MASKED))
            parts.append(scores)
        offset = top * SCALE
        shrink = jnp.exp2((before_top - top) * SCALE)
        total = stats_ref[rows, :1] * shrink
        sums = sums_ref[rows, :] * shrink
        for r in range(2):
            hidden = jnp.where(flag_ref[r + 1] > 0, 0.0, -MASKED)
            more = weigh(parts[r], offset + hidden, got_ref[pieces:, r].reshape(-1, HD))
            sums += more[:, :HD]
            total += more[:, HD:]
        done = (sums / total).astype(jnp.bfloat16)
        for h in range(heads):
            out_ref[c * quarter : (c + 1) * quarter, h * HD : (h + 1) * HD] = done[
                h * quarter : (h + 1) * quarter
            ]


def route_kernel(wanted_ref, held_ref, out_ref):
    for i in range(out_ref.shape[0]):
        out_ref[i] = held_ref[wanted_ref[i]]


VMEM = pl.BlockSpec(memory_space=pltpu.VMEM)
SMEM = pl.BlockSpec(memory_space=pltpu.SMEM)


def call(kernel, out_shape, operands, flops, name):
    return pl.pallas_call(
        kernel,
        out_shape=out_shape,
        in_specs=[SMEM] + [VMEM] * (len(operands) - 1),
        out_specs=[VMEM] * len(out_shape),
        compiler_params=pltpu.CompilerParams(vmem_limit_bytes=40 * 2**20),
        cost_estimate=pl.CostEstimate(flops=flops, bytes_accessed=2**22, transcendentals=2**21),
        name=name,
    )(*operands)


def attend_near(flags, queries, own, before):
    block_len, width = queries.shape
    stacked = block_len * width // HD
    shape = jax.ShapeDtypeStruct((stacked, HD), jnp.float32)
    flops = 8 * stacked * block_len * HD
    return call(near_kernel, [shape, shape], (flags, queries, own, before), flops, "attend_near")


def attend_far(flags, queries, got, sums, stats):
    block_len, width = queries.shape
    shape = jax.ShapeDtypeStruct((block_len, width), jnp.bfloat16)
    flops = 8 * block_len * width * block_len
    return call(far_kernel, [shape], (flags, queries, got, sums, stats), flops, "attend_far")[0]


def route(wanted, held):
    shape = jax.ShapeDtypeStruct(wanted.shape + held.shape[1:], held.dtype)
    return call(route_kernel, [shape], (wanted, held), 2**20, "route")[0]


RING = 4
RIGHT = [(i, (i + 1) % RING) for i in range(RING)]
LEFT = [(i, (i - 1) % RING) for i in range(RING)]
EVEN = [(i, i ^ 1) for i in range(RING)]
ODD = [(i, RING - 1 - i) for i in range(RING)]


def project_out(attended, w_out, w_near, me):
    rows, depth = attended.shape
    quarter, half = rows // RING, w_out.shape[1] // 2
    even, odd = me ^ 1, RING - 1 - me
    parts = attended.reshape(RING, quarter, depth)

    def pick(one, two):
        return jnp.concatenate(
            [
                lax.dynamic_index_in_dim(parts, one, 0, keepdims=False),
                lax.dynamic_index_in_dim(parts, two, 0, keepdims=False),
            ],
            axis=0,
        )

    across = (me + 2) % RING
    got_even = lax.ppermute(pick(even, across), "kvh", EVEN)
    got_odd = lax.ppermute(pick(odd, across), "kvh", ODD)

    def times(rows, w):
        return jnp.dot(rows, w, preferred_element_type=jnp.float32)

    sums_first = times(pick(me, odd), w_out[:, :half]) + times(got_even, w_near[0])
    other_first = lax.ppermute(sums_first[quarter:].astype(jnp.bfloat16), "kvh", ODD)
    sums_second = times(pick(me, even), w_out[:, half:]) + times(got_odd, w_near[1])
    other_second = lax.ppermute(sums_second[quarter:].astype(jnp.bfloat16), "kvh", EVEN)
    return jnp.concatenate(
        [
            (sums_first[:quarter] + other_first.astype(jnp.float32)).astype(jnp.bfloat16),
            (sums_second[:quarter] + other_second.astype(jnp.float32)).astype(jnp.bfloat16),
        ],
        axis=1,
    )


def after(value, *others):
    return lax.optimization_barrier((value, *others))[0]


def local(tokens, norm_gain, w_query, w_key, w_value, w_out, picks):
    me, block_index = lax.axis_index("kvh"), lax.axis_index("ctx")
    ctx_count = lax.axis_size("ctx")
    block_len = tokens.shape[0]
    half = block_len // 2
    chosen = picks[0, 0]

    wanted = lax.all_to_all(
        jnp.broadcast_to(chosen[None, None, 1:], (ctx_count, 1, 2)), "ctx", 0, 0
    ).reshape(ctx_count * 2)

    width = tokens.shape[1]
    from_left = lax.ppermute(tokens, "kvh", RIGHT)
    from_right = lax.ppermute(tokens, "kvh", LEFT)
    positions = block_index * block_len + jnp.arange(block_len, dtype=jnp.int32)
    cosine, sine = turns(positions)
    def weights(w, place):
        start = place % RING * width
        rows = lax.dynamic_slice_in_dim(w, start, width, 0)
        return (rows * lax.dynamic_slice_in_dim(norm_gain, start, width, 0)[:, None]).astype(jnp.bfloat16)

    def times(rows, w):
        return jnp.dot(rows, w, preferred_element_type=jnp.float32)

    w_kv = jnp.concatenate([w_key, w_value], axis=1)
    kv_own = times(tokens, weights(w_kv, me))
    kv_weights = [weights(w_kv, me + step) for step in (3, 1, 2)]
    from_left, from_right, wanted, cosine, kv_own, kv_weights = lax.optimization_barrier(
        (from_left, from_right, wanted, cosine, kv_own, kv_weights)
    )
    upper = lax.ppermute(from_left[:half], "kvh", RIGHT)
    lower = lax.ppermute(from_right[half:], "kvh", LEFT)

    def project(own, left, right, across):
        sofar = own + times(from_left, left) + times(from_right, right)
        return sofar + jnp.concatenate([times(upper, across), times(lower, across)], axis=0)

    def squares(rows):
        return jnp.sum(jnp.square(rows.astype(jnp.float32)), axis=1, keepdims=True)

    square_sum = squares(tokens) + squares(from_left) + squares(from_right)
    square_sum += jnp.concatenate([squares(upper), squares(lower)], axis=0)
    scale = lax.rsqrt(square_sum / (RING * width) + 1e-05)

    kv = project(kv_own, *kv_weights) * scale
    key_rows = rotate_pairs(kv[:, None, :HD], cosine, sine)[:, 0].astype(jnp.bfloat16)
    own = jnp.concatenate([key_rows, kv[:, HD:].astype(jnp.bfloat16)], axis=0)
    held = lax.all_to_all(own.reshape(ctx_count, -1, HD), "ctx", 0, 0)
    before = lax.ppermute(own, "ctx", [(i, i + 1) for i in range(ctx_count - 1)])
    got = lax.all_to_all(route(wanted, held).reshape(ctx_count, 2, -1, HD), "ctx", 0, 0)

    mid = w_out.shape[1] // 2
    passed = after(w_out, from_left)
    front, back = after(passed[:, :mid], upper, lower), after(passed[:, mid:], upper, lower)
    w_near = lax.ppermute(front, "kvh", EVEN), lax.ppermute(back, "kvh", ODD)

    w_late = after(w_query, from_left)
    queries = (project(
        times(tokens, weights(w_late, me)), *(weights(w_late, me + step) for step in (3, 1, 2))
    ) * scale).reshape(block_len, -1, HD)
    queries = rotate_pairs(queries, cosine, sine).astype(jnp.bfloat16).reshape(block_len, -1)
    flags = (chosen < block_index).astype(jnp.int32)
    sums, stats = attend_near(flags, queries, own, before)
    attended = attend_far(flags, queries, got, sums, stats)
    return project_out(attended, w_out, w_near, me)


def solution(mesh):
    in_specs = (
        P("ctx", "kvh"),
        P(),
        P(None, "kvh"),
        P(None, "kvh"),
        P(None, "kvh"),
        P("kvh", None),
        P("ctx", "kvh", None),
    )
    out_specs = P(("ctx", "kvh"), None)
    return jax.shard_map(local, mesh=mesh, in_specs=in_specs, out_specs=out_specs, check_vma=False)
```

```python
import jax
import jax.numpy as jnp
from jax import lax
from jax.experimental import pallas as pl
from jax.experimental.pallas import tpu as pltpu
from jax.sharding import PartitionSpec as P

HD = 128


ROPE_BASE = 500000.0


def turns(positions):
    half_dim = HD // 2
    frequency = ROPE_BASE ** (-jnp.arange(half_dim, dtype=jnp.float32) * 2.0 / HD)
    angles = positions.astype(jnp.float32)[:, None] * frequency[None, :]
    return jnp.cos(angles), jnp.sin(angles)


def rotate_pairs(head_rows, cosine, sine):
    cosine, sine = cosine[:, None, :], sine[:, None, :]
    lower_half = head_rows[..., : HD // 2]
    upper_half = head_rows[..., HD // 2 :]
    return jnp.concatenate(
        [lower_half * cosine - upper_half * sine, upper_half * cosine + lower_half * sine],
        axis=-1,
    )


SCALE = 1.4426950408889634 * HD**-0.5
MASKED = -1e30


def stack_heads(rows):
    return jnp.concatenate(
        [rows[:, h * HD : (h + 1) * HD] for h in range(rows.shape[1] // HD)], axis=0
    )


def scores_of(queries, keys):
    return lax.dot_general(
        queries, keys, (((1,), (1,)), ((), ())), preferred_element_type=jnp.float32
    )


def weigh(scores, offset, values):
    weights = jnp.exp2(scores * SCALE - offset).astype(jnp.bfloat16)
    wide = jnp.concatenate([values, jnp.ones_like(values)], axis=1)
    return jnp.dot(weights, wide, preferred_element_type=jnp.float32)


def row_max(scores):
    return jnp.max(scores, axis=1, keepdims=True)


def near_kernel(flag_ref, query_ref, own_ref, before_ref, sums_ref, stats_ref):
    block_len = query_ref.shape[0]
    quarter = block_len // RING
    heads = query_ref.shape[1] // HD
    stacked = quarter * heads
    has_before = flag_ref[0] > 0
    hidden = jnp.where(has_before, 0.0, -MASKED)
    row = lax.broadcasted_iota(jnp.int32, (stacked, quarter), 0) % quarter
    causal = lax.broadcasted_iota(jnp.int32, (stacked, quarter), 1) <= row
    left = lax.broadcasted_iota(jnp.int32, (stacked, HD), 1) < HD // 2
    for c in range(RING):
        start, end = c * quarter, (c + 1) * quarter
        queries = stack_heads(query_ref[start:end, :])
        own_scores = jnp.where(causal, scores_of(queries, own_ref[start:end, :]), MASKED)
        before_scores = scores_of(queries, before_ref[:block_len, :])
        top = jnp.maximum(
            row_max(own_scores), jnp.where(has_before, row_max(before_scores), MASKED)
        )
        if c:
            early_scores = scores_of(queries, own_ref[:start, :])
            top = jnp.maximum(top, row_max(early_scores))
        offset = top * SCALE
        sums = weigh(own_scores, offset, own_ref[block_len + start : block_len + end, :])
        sums += weigh(before_scores, offset + hidden, before_ref[block_len:, :])
        if c:
            sums += weigh(early_scores, offset, own_ref[block_len : block_len + start, :])
        rows = slice(c * stacked, (c + 1) * stacked)
        sums_ref[rows, :] = sums[:, :HD]
        stats_ref[rows, :] = jnp.where(left, sums[:, HD:], top)


def far_kernel(flag_ref, query_ref, got_ref, sums_ref, stats_ref, out_ref):
    block_len, width = query_ref.shape
    quarter = block_len // RING
    heads = width // HD
    stacked = quarter * heads
    pieces = got_ref.shape[0] // 2
    for c in range(RING):
        rows = slice(c * stacked, (c + 1) * stacked)
        queries = stack_heads(query_ref[c * quarter : (c + 1) * quarter, :])
        before_top = stats_ref[rows, HD // 2 : HD // 2 + 1]
        top, parts = before_top, []
        for r in range(2):
            scores = scores_of(queries, got_ref[:pieces, r].reshape(-1, HD))
            top = jnp.maximum(top, jnp.where(flag_ref[r + 1] > 0, row_max(scores), MASKED))
            parts.append(scores)
        offset = top * SCALE
        shrink = jnp.exp2((before_top - top) * SCALE)
        total = stats_ref[rows, :1] * shrink
        sums = sums_ref[rows, :] * shrink
        for r in range(2):
            hidden = jnp.where(flag_ref[r + 1] > 0, 0.0, -MASKED)
            more = weigh(parts[r], offset + hidden, got_ref[pieces:, r].reshape(-1, HD))
            sums += more[:, :HD]
            total += more[:, HD:]
        done = (sums / total).astype(jnp.bfloat16)
        for h in range(heads):
            out_ref[c * quarter : (c + 1) * quarter, h * HD : (h + 1) * HD] = done[
                h * quarter : (h + 1) * quarter
            ]


def route_kernel(wanted_ref, held_ref, out_ref):
    for i in range(out_ref.shape[0]):
        out_ref[i] = held_ref[wanted_ref[i]]


VMEM = pl.BlockSpec(memory_space=pltpu.VMEM)
SMEM = pl.BlockSpec(memory_space=pltpu.SMEM)


def call(kernel, out_shape, operands, flops, name):
    return pl.pallas_call(
        kernel,
        out_shape=out_shape,
        in_specs=[SMEM] + [VMEM] * (len(operands) - 1),
        out_specs=[VMEM] * len(out_shape),
        compiler_params=pltpu.CompilerParams(vmem_limit_bytes=40 * 2**20),
        cost_estimate=pl.CostEstimate(flops=flops, bytes_accessed=2**22, transcendentals=2**21),
        name=name,
    )(*operands)


def attend_near(flags, queries, own, before):
    block_len, width = queries.shape
    stacked = block_len * width // HD
    shape = jax.ShapeDtypeStruct((stacked, HD), jnp.float32)
    flops = 8 * stacked * block_len * HD
    return call(near_kernel, [shape, shape], (flags, queries, own, before), flops, "attend_near")


def attend_far(flags, queries, got, sums, stats):
    block_len, width = queries.shape
    shape = jax.ShapeDtypeStruct((block_len, width), jnp.bfloat16)
    flops = 8 * block_len * width * block_len
    return call(far_kernel, [shape], (flags, queries, got, sums, stats), flops, "attend_far")[0]


def route(wanted, held):
    shape = jax.ShapeDtypeStruct(wanted.shape + held.shape[1:], held.dtype)
    return call(route_kernel, [shape], (wanted, held), 2**20, "route")[0]


RING = 4
RIGHT = [(i, (i + 1) % RING) for i in range(RING)]
LEFT = [(i, (i - 1) % RING) for i in range(RING)]
EVEN = [(i, i ^ 1) for i in range(RING)]
ODD = [(i, RING - 1 - i) for i in range(RING)]


def project_out(attended, w_out, w_near, me, core):
    rows, depth = attended.shape
    quarter, half = rows // RING, w_out.shape[1] // 2
    even, odd = me ^ 1, RING - 1 - me
    parts = attended.reshape(RING, quarter, depth)

    def pick(one, two, parts=parts):
        return jnp.concatenate(
            [
                lax.dynamic_index_in_dim(parts, one, 0, keepdims=False),
                lax.dynamic_index_in_dim(parts, two, 0, keepdims=False),
            ],
            axis=0,
        )

    across = (me + 2) % RING
    turned = jnp.concatenate([parts[..., depth // 2 :], parts[..., : depth // 2]], axis=-1)
    turned = jnp.where(core == 0, parts, turned)
    got_even = lax.ppermute(pick(even, across, turned), "kvh", EVEN)
    got_odd = lax.ppermute(pick(odd, across, turned), "kvh", ODD)

    def times(rows, w):
        return jnp.dot(rows, w, preferred_element_type=jnp.float32)

    sums_first = times(pick(me, odd), w_out[:, :half]) + times(got_even, w_near[0])
    other_first = lax.ppermute(sums_first[quarter:].astype(jnp.bfloat16), "kvh", ODD)
    sums_second = times(pick(me, even), w_out[:, half:]) + times(got_odd, w_near[1])
    other_second = lax.ppermute(sums_second[quarter:].astype(jnp.bfloat16), "kvh", EVEN)
    return jnp.concatenate(
        [
            (sums_first[:quarter] + other_first.astype(jnp.float32)).astype(jnp.bfloat16),
            (sums_second[:quarter] + other_second.astype(jnp.float32)).astype(jnp.bfloat16),
        ],
        axis=1,
    )


def after(value, *others):
    return lax.optimization_barrier((value, *others))[0]


def local(tokens, norm_gain, w_query, w_key, w_value, w_out, picks):
    me, block_index = lax.axis_index("kvh"), lax.axis_index("ctx")
    ctx_count = lax.axis_size("ctx")
    block_len = tokens.shape[0]
    half = block_len // 2
    chosen = picks[0, 0]

    wanted = lax.all_to_all(
        jnp.broadcast_to(chosen[None, None, 1:], (ctx_count, 1, 2)), "ctx", 0, 0
    ).reshape(ctx_count * 2)

    width = tokens.shape[1]
    from_left = lax.ppermute(tokens, "kvh", RIGHT)
    from_right = lax.ppermute(tokens, "kvh", LEFT)
    positions = block_index * block_len + jnp.arange(block_len, dtype=jnp.int32)
    cosine, sine = turns(positions)
    def weights(w, place):
        start = place % RING * width
        rows = lax.dynamic_slice_in_dim(w, start, width, 0)
        return (rows * lax.dynamic_slice_in_dim(norm_gain, start, width, 0)[:, None]).astype(jnp.bfloat16)

    def times(rows, w):
        return jnp.dot(rows, w, preferred_element_type=jnp.float32)

    w_kv = jnp.concatenate([w_key, w_value], axis=1)
    kv_own = times(tokens, weights(w_kv, me))
    kv_weights = [weights(w_kv, me + step) for step in (3, 1, 2)]
    from_left, from_right, wanted, cosine, kv_own, kv_weights = lax.optimization_barrier(
        (from_left, from_right, wanted, cosine, kv_own, kv_weights)
    )
    upper = lax.ppermute(from_left[:half], "kvh", RIGHT)
    lower = lax.ppermute(from_right[half:], "kvh", LEFT)

    def project(own, left, right, across):
        sofar = own + times(from_left, left) + times(from_right, right)
        return sofar + jnp.concatenate([times(upper, across), times(lower, across)], axis=0)

    def squares(rows):
        return jnp.sum(jnp.square(rows.astype(jnp.float32)), axis=1, keepdims=True)

    square_sum = squares(tokens) + squares(from_left) + squares(from_right)
    square_sum += jnp.concatenate([squares(upper), squares(lower)], axis=0)
    scale = lax.rsqrt(square_sum / (RING * width) + 1e-05)

    kv = project(kv_own, *kv_weights) * scale
    key_rows = rotate_pairs(kv[:, None, :HD], cosine, sine)[:, 0].astype(jnp.bfloat16)
    own = jnp.concatenate([key_rows, kv[:, HD:].astype(jnp.bfloat16)], axis=0)
    held = lax.all_to_all(own.reshape(ctx_count, -1, HD), "ctx", 0, 0)
    before = lax.ppermute(own, "ctx", [(i, i + 1) for i in range(ctx_count - 1)])
    got = lax.all_to_all(route(wanted, held).reshape(ctx_count, 2, -1, HD), "ctx", 0, 0)

    mid, core = w_out.shape[1] // 2, block_index % 2
    passed = after(w_out, from_left)
    passed = lax.dynamic_slice_in_dim(passed, core * (passed.shape[0] // 2), passed.shape[0] // 2, 0)
    front, back = after(passed[:, :mid], upper, lower), after(passed[:, mid:], upper, lower)
    cores = [(i, i ^ 1) for i in range(ctx_count)]
    w_near = [lax.ppermute(front, "kvh", EVEN), lax.ppermute(back, "kvh", ODD)]
    w_near = [jnp.concatenate([w, lax.ppermute(w, "ctx", cores)], axis=0) for w in w_near]

    w_late = after(w_query, from_left)
    queries = (project(
        times(tokens, weights(w_late, me)), *(weights(w_late, me + step) for step in (3, 1, 2))
    ) * scale).reshape(block_len, -1, HD)
    queries = rotate_pairs(queries, cosine, sine).astype(jnp.bfloat16).reshape(block_len, -1)
    flags = (chosen < block_index).astype(jnp.int32)
    sums, stats = attend_near(flags, queries, own, before)
    attended = attend_far(flags, queries, got, sums, stats)
    return project_out(attended, w_out, w_near, me, core)


def solution(mesh):
    in_specs = (
        P("ctx", "kvh"),
        P(),
        P(None, "kvh"),
        P(None, "kvh"),
        P(None, "kvh"),
        P("kvh", None),
        P("ctx", "kvh", None),
    )
    out_specs = P(("ctx", "kvh"), None)
    return jax.shard_map(local, mesh=mesh, in_specs=in_specs, out_specs=out_specs, check_vma=False)
```
